32 devices in a mesh: sta: 4 (over y, core), src: 8 (over z, x).
Axes of the slice: x: 2, y: 2, z: 4, core: 2. Of those that a mesh axis runs over, the one named last changes fastest.
Arguments:
- features: bfloat16 [128, 256, 128], P('sta', 'src'), may hold values from -6 to 6
- station_lists: int32 [128, 16], replicated, may hold values from 0 to 127, as said below
- station_counts: int32 [128], replicated, may hold values from 1 to 16
- source_lists: int32 [256, 16], replicated, may hold values from 0 to 255, as said below
- source_counts: int32 [256], replicated, may hold values from 1 to 16
- picks: int32 [2, 128], P(None, 'sta'), may hold values 0 or 1
- targets: float32 [2, 256], P(None, 'src'), may hold values from 0 to 1
- layer_weights: bfloat16 [2, 3, 64, 64], replicated, may hold values from -0.75 to 0.75
- readout_vector: bfloat16 [64], replicated, may hold values from -0.75 to 0.75
Outputs:
- likelihood: float32 [2, 256], P(None, 'src')
- feature_grad: bfloat16 [128, 256, 128], P('sta', 'src')
- weight_grad: float32 [2, 3, 64, 64], replicated
- vector_grad: float32 [64], replicated
The draws below stay inside these ranges and needn't reach their ends.
Inputs may be any that keep to these rules, and one draw needn't show every extreme that they name: `station_lists`: every entry of a station's list lies within 16 rows of that station; entries past its count are padding. `source_lists`: every entry of a source node's list lies within 16 rows of that source node; entries past its count are padding.
All inputs are finite; a program needn't handle non-finite values. No bound on the sum of `picks` on one device may be relied on, other than what follows from the above.
Results may differ from the reference program's by a relative error of at most 0.015.
Values may be sent and summed in bfloat16 or wider, within the bound.
A program may use at most 64 MiB of HBM per device.

```python
import jax
import jax.numpy as jnp
from jax import lax

F = 64
W = 2
LAYERS = 2
KS = 16
KR = 16
HW = 16
NSTA = 128
NSRC = 256


def neighbour_table(key, row_count, list_width):
    key_span, key_sign = jax.random.split(key)
    span_sizes = jax.random.randint(key_span, (row_count, list_width), 1, HW + 1)
    sign_bits = jax.random.randint(key_sign, (row_count, list_width), 0, 2) * 2 - 1
    offsets = span_sizes * sign_bits
    own_rows = jnp.arange(row_count, dtype=jnp.int32)[:, None]
    edge_step = jnp.where(own_rows % 2 == 0, HW, -HW)
    offsets = offsets.at[:, 0:1].set(edge_step)
    return jnp.clip(own_rows + offsets, 0, row_count - 1).astype(jnp.int32)


def neighbour_counts(key, row_count, list_width):
    counts = jax.random.randint(key, (row_count,), 1, list_width + 1)
    return counts.at[0].set(list_width).at[1].set(1).astype(jnp.int32)


def draw_station_lists(key, part):
    return neighbour_table(jax.random.fold_in(key, 11), NSTA, KS)


def draw_station_counts(key, part):
    return neighbour_counts(jax.random.fold_in(key, 12), NSTA, KS)


def draw_source_lists(key, part):
    return neighbour_table(jax.random.fold_in(key, 13), NSRC, KR)


def draw_source_counts(key, part):
    return neighbour_counts(jax.random.fold_in(key, 14), NSRC, KR)


def plant(drawn, own_key, least, largest):
    dims = drawn.shape
    spot = [jax.random.randint(jax.random.fold_in(own_key, axis), (), 0, dims[axis]) for axis in range(len(dims))]
    drawn = drawn.at[tuple(spot)].set(least)
    longest = dims.index(max(dims))
    spot[longest] = (spot[longest] + 1) % dims[longest]
    return drawn.at[tuple(spot)].set(largest)


def steps_of(own_key, shape, shards, low, high):
    loudness, own = 1.0, jax.random.fold_in(own_key, 6)
    for dim, blocks in shards:
        draws = jnp.exp(jax.random.uniform(jax.random.fold_in(own, dim), (blocks,), jnp.float32, low / len(shards), high / len(shards)))
        loudness = loudness * jnp.repeat(draws, shape[dim] // blocks).reshape([-1 if axis == dim else 1 for axis in range(len(shape))])
    return loudness


def bell_draw(rng, extent, width, limit, pieces=(), kind=jnp.bfloat16):
    drawn = jax.random.normal(rng, extent, jnp.float32) * width
    if len(pieces) > 0:
        drawn = steps_of(rng, extent, pieces, -0.22, 0.18) * drawn
    return jnp.clip(drawn, min=-limit, max=limit).astype(kind)


def setup_inputs(seed: int = 0) -> dict:
    key_list = jax.random.split(jax.random.key(seed), 10)
    return {
        "features": bell_draw(key_list[0], (NSTA, NSRC, W * F), 1.0, 6.0, ((0, 4), (1, 8))),
        "station_lists": draw_station_lists(jax.random.fold_in(key_list[9], 71), 0),
        "station_counts": draw_station_counts(jax.random.fold_in(key_list[9], 71), 0),
        "source_lists": draw_source_lists(jax.random.fold_in(key_list[9], 71), 0),
        "source_counts": draw_source_counts(jax.random.fold_in(key_list[9], 71), 0),
        "picks": plant((jax.random.randint(key_list[5], (W, NSTA), 0, 2) < 1).astype(jnp.int32), jax.random.fold_in(key_list[5], 1), 0, 1),
        "targets": jnp.clip(1.0 * jax.random.uniform(key_list[6], (W, NSRC), jnp.float32) ** steps_of(key_list[6], (W, NSRC), ((1, 8),), -0.2, 0.2), 0.0, 1.0),
        "layer_weights": bell_draw(key_list[7], (LAYERS, 3, F, F), F ** -0.5, 0.75),
        "readout_vector": bell_draw(key_list[8], (F,), F ** -0.5, 0.75),
    }


def window_product(values, matrix):
    feature = matrix.shape[0]
    flat = values.reshape(-1, feature)
    return jnp.dot(flat, matrix, preferred_element_type=jnp.float32).reshape(values.shape)

def station_mix(states, lists, counts):
    running = jnp.zeros(states.shape, jnp.float32)
    for column in range(KS):
        kept_rows = (column < counts).astype(jnp.float32)[:, None, None]
        running = running + kept_rows * states[lists[:, column]].astype(jnp.float32)
    return running / counts.astype(jnp.float32)[:, None, None]

def source_mix(states, lists, counts):
    running = jnp.zeros(states.shape, jnp.float32)
    for column in range(KR):
        kept_rows = (column < counts).astype(jnp.float32)[None, :, None]
        running = running + kept_rows * states[:, lists[:, column]].astype(jnp.float32)
    return running / counts.astype(jnp.float32)[None, :, None]

def station_back(cotangent, lists, counts):
    running = jnp.zeros(cotangent.shape, jnp.float32)
    for column in range(KS):
        kept_rows = (column < counts).astype(jnp.float32)[:, None, None]
        running = running.at[lists[:, column]].add(kept_rows * cotangent.astype(jnp.float32))
    return running

def source_back(cotangent, lists, counts):
    running = jnp.zeros(cotangent.shape, jnp.float32)
    for column in range(KR):
        kept_rows = (column < counts).astype(jnp.float32)[None, :, None]
        running = running.at[:, lists[:, column]].add(kept_rows * cotangent.astype(jnp.float32))
    return running

def layer_parts(states, weights, station_lists, station_counts, source_lists, source_counts):
    sta_mean = station_mix(states, station_lists, station_counts).astype(jnp.bfloat16)
    src_mean = source_mix(states, source_lists, source_counts).astype(jnp.bfloat16)
    linear = window_product(states, weights[0]) + window_product(sta_mean, weights[1]) + window_product(src_mean, weights[2])
    return (sta_mean, src_mean, jnp.tanh(linear))

def outer_sum(left, right, feature):
    return jnp.dot(left.reshape(-1, feature).T, right.reshape(-1, feature), preferred_element_type=jnp.float32)

def reference(features, station_lists, station_counts, source_lists, source_counts, picks, targets, layer_weights, readout_vector):
    feature = layer_weights.shape[-1]
    windows = features.shape[2] // feature
    states = features
    history = []
    for layer_idx in range(LAYERS):
        history.append(states)
        sta_mean, src_mean, squashed = layer_parts(states, layer_weights[layer_idx], station_lists, station_counts, source_lists, source_counts)
        states = (states.astype(jnp.float32) + squashed).astype(jnp.bfloat16)
    score = jnp.dot(states.reshape(-1, feature), readout_vector, preferred_element_type=jnp.float32)
    score = score.reshape(NSTA, NSRC, windows)
    picked = picks.astype(jnp.float32)
    root = jnp.sqrt(jnp.maximum(lax.optimization_barrier(jnp.sum(picked, axis=1)), 1.0))
    summed = lax.optimization_barrier(jnp.sum(picked.T[:, None, :] * score, axis=0)).T
    likelihood = summed / root[:, None]
    error = jax.nn.sigmoid(likelihood) - targets
    d_score = (picked.T[:, None, :] * error.T[None, :, :]).astype(jnp.bfloat16)
    v_sum = jnp.einsum('nw,nwf->f', d_score.reshape(-1, windows).astype(jnp.float32), states.reshape(-1, windows, feature).astype(jnp.float32), precision=lax.Precision.HIGHEST)
    grad = (d_score.astype(jnp.float32)[..., None] * readout_vector.astype(jnp.float32)).reshape(states.shape)
    w_rows = []
    for layer_idx in reversed(range(LAYERS)):
        weights = layer_weights[layer_idx]
        before = history[layer_idx]
        sta_mean, src_mean, squashed = layer_parts(before, weights, station_lists, station_counts, source_lists, source_counts)
        delta = (grad * (1.0 - squashed * squashed)).astype(jnp.bfloat16)
        w_rows.append(jnp.stack([outer_sum(before, delta, feature), outer_sum(sta_mean, delta, feature), outer_sum(src_mean, delta, feature)]))
        u_sta = (window_product(delta, weights[1].T) / station_counts.astype(jnp.float32)[:, None, None]).astype(jnp.bfloat16)
        u_src = (window_product(delta, weights[2].T) / source_counts.astype(jnp.float32)[None, :, None]).astype(jnp.bfloat16)
        grad = grad + window_product(delta, weights[0].T) + station_back(u_sta, station_lists, station_counts) + source_back(u_src, source_lists, source_counts)
    w_sum = jnp.stack(w_rows[::-1])
    factor = 1.0 / jnp.sqrt(jnp.float32(NSTA) * jnp.float32(NSRC))
    return (likelihood, grad.astype(jnp.bfloat16), w_sum * factor, v_sum * factor)
```

```python
import functools

import jax
import jax.numpy as jnp
from jax import lax
from jax.experimental import pallas as pl
from jax.experimental.pallas import tpu as pltpu
from jax.sharding import PartitionSpec as P

LAYERS = 2
HW = 16
J = 16
G = 4
MESH = pl.DeviceIdType.MESH
F32, BF16 = jnp.float32, jnp.bfloat16


def iota(shape, dim):
    return lax.broadcasted_iota(jnp.int32, shape, dim)


def ones_where(cond):
    return jnp.where(cond, 1.0, 0.0).astype(BF16)


def dot(a, b):
    return lax.dot_general(a, b, (((1,), (0,)), ((), ())), preferred_element_type=F32)


def dot_nt(a, b):
    return lax.dot_general(a, b, (((1,), (1,)), ((), ())), preferred_element_type=F32)


def dot_tn(a, b):
    return lax.dot_general(a, b, (((0,), (0,)), ((), ())), preferred_element_type=F32)


def coefs(list_ref, count_row, start, rows, base, span):
    start = pl.multiple_of(start, HW)
    lists = list_ref[pl.ds(start, rows), :] - base
    lanes = iota((rows, count_row.shape[1]), 1)
    own = iota((rows, count_row.shape[1]), 0) + start
    count = jnp.sum(jnp.where(lanes == own, count_row, 0.0), axis=1, keepdims=True)
    place = iota((rows, span), 1)
    total = jnp.zeros((rows, span), F32)
    for k in range(lists.shape[1]):
        hit = (lists[:, k : k + 1] == place) & (count > float(k))
        total = total + jnp.where(hit, 1.0, 0.0)
    return (total / count).astype(BF16)


def halo_coefs(list_ref, count_row, first, rows, total_rows):
    before = lax.rem(first + total_rows - HW, total_rows)
    after = lax.rem(first + rows, total_rows)
    return jnp.concatenate(
        [
            coefs(list_ref, count_row, before, HW, first, rows),
            coefs(list_ref, count_row, first, rows, first, rows),
            coefs(list_ref, count_row, after, HW, first, rows),
        ],
        axis=0,
    )


def kernel(
    n_sta,
    n_src,
    chunk,
    feat,
    slist,
    scnt,
    rlist,
    rcnt,
    picks,
    targets,
    weights,
    readout,
    lik_out,
    grad_out,
    w_out,
    hs,
    hr,
    x,
    xb,
    slope,
    ks,
    bd,
    wf,
    q,
    qt,
    lik_slots,
    w_local,
    sta_slots,
    src_slots,
    total,
    halo_send,
    halo_recv,
    lik_send,
    lik_recv,
    a_send,
    a_recv,
    b_send,
    b_recv,
    c_send,
    c_recv,
):
    me_sta = lax.axis_index("sta")
    me_src = lax.axis_index("src")
    rows, cols, lanes = feat.shape
    feature = weights.shape[-1]
    windows = lanes // feature
    span_s, span_r = rows + 2 * HW, cols + 2 * HW
    nodes = rows * cols
    sta_first, src_first = me_sta * rows, me_src * cols

    def sta_peer(d):
        return lax.rem(me_sta + d, n_sta)

    def src_peer(d):
        return lax.rem(me_src + d, n_src)

    for e in range(2 * LAYERS):
        zero_s = jnp.zeros((HW, cols, lanes), BF16)
        zero_r = jnp.zeros((rows, HW, lanes), BF16)

        @pl.when(me_sta == 0)
        def _():
            hs[e, 0:HW] = zero_s

        @pl.when(me_sta == n_sta - 1)
        def _():
            hs[e, HW + rows :] = zero_s

        @pl.when(me_src == 0)
        def _():
            hr[e, :, 0:HW] = zero_r

        @pl.when(me_src == n_src - 1)
        def _():
            hr[e, :, HW + cols :] = zero_r

    barrier = pltpu.get_barrier_semaphore()
    for d in range(1, n_sta):
        pl.semaphore_signal(barrier, inc=1, device_id={"sta": sta_peer(d)}, device_id_type=MESH)
    for d in range(1, n_src):
        pl.semaphore_signal(barrier, inc=1, device_id={"src": src_peer(d)}, device_id_type=MESH)
    pl.semaphore_wait(barrier, n_sta + n_src - 2)

    def halo_copy(e, direction):
        if direction == 0:
            src, dst, device = hs.at[e, HW : 2 * HW], hs.at[e, HW + rows :], {"sta": me_sta - 1}
        elif direction == 1:
            src, dst, device = hs.at[e, rows : HW + rows], hs.at[e, 0:HW], {"sta": me_sta + 1}
        elif direction == 2:
            src, dst, device = hr.at[e, :, HW : 2 * HW], hr.at[e, :, HW + cols :], {"src": me_src - 1}
        else:
            src, dst, device = hr.at[e, :, cols : HW + cols], hr.at[e, :, 0:HW], {"src": me_src + 1}
        return pltpu.make_async_remote_copy(
            src_ref=src,
            dst_ref=dst,
            send_sem=halo_send.at[e, direction],
            recv_sem=halo_recv.at[e, direction],
            device_id=device,
            device_id_type=MESH,
        )

    has = [me_sta > 0, me_sta < n_sta - 1, me_src > 0, me_src < n_src - 1]

    def halo_start(e, values):
        hr[e, :, HW : HW + cols] = values
        for direction in (2, 3):
            pl.when(has[direction])(lambda: halo_copy(e, direction).start())
        hs[e, HW : HW + rows] = values
        for direction in (0, 1):
            pl.when(has[direction])(lambda: halo_copy(e, direction).start())

    def halo_wait(e, directions):
        for direction in directions:
            pl.when(has[direction ^ 1])(lambda: halo_copy(e, direction).wait_recv())

    def halo_drain(e):
        for direction in range(4):
            pl.when(has[direction])(lambda: halo_copy(e, direction).wait_send())

    states = feat[...]
    halo_start(0, states)

    s_row, r_row = scnt[...].astype(F32), rcnt[...].astype(F32)
    up_rows = ones_where((iota((rows * J, rows), 0) // J) == iota((rows * J, rows), 1))
    up_cols = ones_where((iota((span_s, span_s * J), 1) // J) == iota((span_s, span_s * J), 0))
    rep_rows = ones_where((iota((G * cols, cols), 0) % cols) == iota((G * cols, cols), 1))
    rep_cols = ones_where((iota((span_r, G * span_r), 1) % span_r) == iota((span_r, G * span_r), 0))
    same_col = (iota((rows * J, span_s * J), 0) % J) == (iota((rows * J, span_s * J), 1) % J)
    same_grp = (iota((G * cols, G * span_r), 0) // cols) == (iota((G * cols, G * span_r), 1) // span_r)

    def put_mixes(way, sta_part, src_part):
        wide = dot(sta_part.astype(BF16), up_cols)
        ks[way] = jnp.where(same_col, wide, 0.0).astype(BF16)
        wide = dot(src_part.astype(BF16), rep_cols)
        bd[way] = jnp.where(same_grp, wide, 0.0).astype(BF16)

    fwd_s = coefs(slist, s_row, sta_first, rows, sta_first - HW, span_s)
    fwd_r = coefs(rlist, r_row, src_first, cols, src_first - HW, span_r)
    put_mixes(0, dot(up_rows, fwd_s), dot(rep_rows, fwd_r))

    spread = ones_where((iota((lanes, feature), 0) % feature) == iota((lanes, feature), 1))
    same_win = (iota((lanes, lanes), 0) // feature) == (iota((lanes, lanes), 1) // feature)

    def put_weights(way):
        for l in range(LAYERS):
            for p in range(3):
                m = weights[l, p]
                left = (dot(spread, m) if way == 0 else dot_nt(spread, m)).astype(BF16)
                wide = jnp.where(same_win, dot_nt(left, spread), 0.0)
                wf[way, l, p * lanes : (p + 1) * lanes, :] = wide.astype(BF16)

    put_weights(0)

    def mix_sta(way, e, out):
        for half in range(cols // J):
            part = hs[e, :, half * J : (half + 1) * J, :].reshape(span_s * J, lanes)
            mixed = dot(ks[way], part).astype(BF16)
            out[:, half * J : (half + 1) * J, lanes : 2 * lanes] = mixed.reshape(rows, J, lanes)

    def mix_src(way, e, out):
        for g in range(rows // G):
            part = hr[e, g * G : (g + 1) * G].reshape(G * span_r, lanes)
            mixed = dot(bd[way], part).astype(BF16)
            out[g * G : (g + 1) * G, :, 2 * lanes :] = mixed.reshape(G, cols, lanes)

    wide_readout = dot_nt(readout[...], spread)
    jw = windows * cols
    node_own = iota((jw, lanes), 0)
    win_mask = (node_own // cols) == (iota((jw, lanes), 1) // feature)
    diag = (node_own % cols) == iota((jw, lanes), 1)

    def to_column(row_of):
        wide = jnp.concatenate(
            [jnp.broadcast_to(row_of(w), (cols, lanes)) for w in range(windows)], axis=0
        )
        return jnp.sum(jnp.where(diag, wide, 0.0), axis=1, keepdims=True)

    for l in range(LAYERS):
        x[l, :, :, 0:lanes] = states
        if l == 1:
            t = halo_coefs(slist, s_row, sta_first, rows, n_sta * rows)
            u = halo_coefs(rlist, r_row, src_first, cols, n_src * cols)
            put_mixes(1, dot_nt(up_rows, t), dot_nt(rep_rows, u))
            put_weights(1)
            picked = picks[...].astype(F32)
            wide_picks = jnp.concatenate(
                [jnp.broadcast_to(picked[w : w + 1], (cols, rows)) for w in range(windows)], axis=0
            ).astype(BF16)
            sel = ones_where((iota((nodes, rows), 0) // cols) == iota((nodes, rows), 1))
            at_q = (iota((jw, nodes), 0) % cols) == (iota((jw, nodes), 1) % cols)
            q[...] = jnp.where(at_q, dot_nt(wide_picks, sel), 0.0).astype(BF16)
            at_t = (iota((nodes, jw), 0) % cols) == (iota((nodes, jw), 1) % cols)
            qt[...] = jnp.where(at_t, dot_nt(sel, wide_picks), 0.0).astype(BF16)
        halo_wait(l, (0, 1))
        mix_sta(0, l, x.at[l])
        halo_wait(l, (2, 3))
        mix_src(0, l, x.at[l])
        z = dot(x[l].reshape(nodes, 3 * lanes), wf[0, l])
        squashed = jnp.tanh(z)
        slope[l] = 1.0 - squashed * squashed
        states = (states.astype(F32) + squashed.reshape(rows, cols, lanes)).astype(BF16)
        if l + 1 < LAYERS:
            halo_start(l + 1, states)

    heap = dot(q[...], states.reshape(nodes, lanes))
    score = jnp.sum(jnp.where(win_mask, heap * wide_readout, 0.0), axis=1, keepdims=True)
    flat = jnp.where(diag, score, 0.0)
    tile_row = iota((8, lanes), 0)
    tile = jnp.zeros((8, lanes), F32)
    for w in range(windows):
        part = jnp.sum(flat[w * cols : (w + 1) * cols], axis=0, keepdims=True)
        tile = jnp.where(tile_row == w, part, tile)
        count = jnp.sum(picked[w : w + 1], axis=1, keepdims=True)
        tile = jnp.where(tile_row == windows + w, count, tile)
    lik_slots[me_sta] = tile
    sends = []
    for d in range(1, n_sta):
        sends.append(
            pltpu.make_async_remote_copy(
                src_ref=lik_slots.at[me_sta],
                dst_ref=lik_slots.at[me_sta],
                send_sem=lik_send.at[d],
                recv_sem=lik_recv.at[d],
                device_id={"sta": sta_peer(d)},
                device_id_type=MESH,
            )
        )
        sends[-1].start()
    for copy in sends:
        copy.wait_recv()
    summed = lik_slots[0]
    for s in range(1, n_sta):
        summed = summed + lik_slots[s]
    root = jnp.sqrt(jnp.maximum(summed[windows : 2 * windows], 1.0))
    lik = summed[0:windows] / root
    lik_out[...] = lik[:, :cols]
    sig = jax.nn.sigmoid(lik)
    sig_col = to_column(lambda w: sig[w : w + 1])
    want = jnp.concatenate(
        [jnp.broadcast_to(targets[w : w + 1, :], (cols, cols)) for w in range(windows)], axis=0
    )
    diag_cols = (iota((jw, cols), 0) % cols) == iota((jw, cols), 1)
    want_col = jnp.sum(jnp.where(diag_cols, want, 0.0), axis=1, keepdims=True)
    err = (sig_col - want_col).astype(BF16).astype(F32)
    err_wide = jnp.where(win_mask, err, 0.0)
    v_row = jnp.sum(err_wide * heap, axis=0, keepdims=True)
    grad = dot(qt[...], err_wide.astype(BF16)) * wide_readout

    low = iota((feature, lanes), 1) < feature

    for l in reversed(range(LAYERS)):
        e = 2 * LAYERS - 1 - l
        delta = (grad * slope[l]).astype(BF16)
        delta3 = delta.reshape(rows, cols, lanes)
        halo_start(e, delta3)
        xb[:, :, 0:lanes] = delta3
        w_t = dot_tn(delta, x[l].reshape(nodes, 3 * lanes))
        folded = []
        for p in range(3):
            both = jnp.where(
                low,
                w_t[0:feature, p * lanes : (p + 1) * lanes],
                w_t[feature:, p * lanes : (p + 1) * lanes],
            )
            folded.append(both + pltpu.roll(both, feature, 1))
        w_local[l * feature : (l + 1) * feature] = jnp.where(low, folded[0], folded[1])
        if l == 1:
            kept = folded[2]
        else:
            w_local[2 * feature : 3 * feature] = jnp.where(low, folded[2], kept)
            w_local[3 * feature :] = jnp.broadcast_to(v_row, (w_local.shape[0] - 3 * feature, lanes))
        halo_wait(e, (0, 1))
        mix_sta(1, e, xb)
        halo_wait(e, (2, 3))
        mix_src(1, e, xb)
        grad = grad + dot(xb[...].reshape(nodes, 3 * lanes), wf[1, l])
    grad_out[...] = grad.reshape(rows, cols, lanes).astype(BF16)

    def part(ref, s):
        return ref.at[pl.ds(pl.multiple_of(s * chunk, 8), chunk)]

    first = []
    for d in range(1, n_sta):
        first.append(
            pltpu.make_async_remote_copy(
                src_ref=part(w_local, sta_peer(d)),
                dst_ref=sta_slots.at[me_sta],
                send_sem=a_send.at[d],
                recv_sem=a_recv.at[d],
                device_id={"sta": sta_peer(d)},
                device_id_type=MESH,
            )
        )
        first[-1].start()
    sta_slots[me_sta] = part(w_local, me_sta)[...]
    for copy in first:
        copy.wait_recv()
    some = sta_slots[0]
    for s in range(1, n_sta):
        some = some + sta_slots[s]
    src_slots[me_src] = some
    second = []
    for d in range(1, n_src):
        second.append(
            pltpu.make_async_remote_copy(
                src_ref=src_slots.at[me_src],
                dst_ref=src_slots.at[me_src],
                send_sem=b_send.at[d],
                recv_sem=b_recv.at[d],
                device_id={"src": src_peer(d)},
                device_id_type=MESH,
            )
        )
        second[-1].start()
    for copy in second:
        copy.wait_recv()
    some = src_slots[0]
    for s in range(1, n_src):
        some = some + src_slots[s]
    part(total, me_sta)[...] = some
    third = []
    for d in range(1, n_sta):
        third.append(
            pltpu.make_async_remote_copy(
                src_ref=part(total, me_sta),
                dst_ref=part(total, me_sta),
                send_sem=c_send.at[d],
                recv_sem=c_recv.at[d],
                device_id={"sta": sta_peer(d)},
                device_id_type=MESH,
            )
        )
        third[-1].start()
    for e in range(2 * LAYERS):
        halo_drain(e)
    for copy in third:
        copy.wait_recv()
    w_out[...] = total[...]
    for copy in sends + first + second + third:
        copy.wait_send()


def shards(
    n_sta,
    n_src,
    features,
    station_lists,
    station_counts,
    source_lists,
    source_counts,
    picks,
    targets,
    layer_weights,
    readout_vector,
):
    rows, cols, lanes = features.shape
    feature = layer_weights.shape[-1]
    windows = lanes // feature
    nodes = rows * cols
    span_s, span_r = rows + 2 * HW, cols + 2 * HW
    chunk = -(-(3 * feature + 1) // (8 * n_sta)) * 8
    w_rows = chunk * n_sta
    jw = windows * cols
    dma = pltpu.SemaphoreType.DMA
    vmem = pl.BlockSpec(memory_space=pltpu.VMEM)
    lik, grad, w_sum = pl.pallas_call(
        functools.partial(kernel, n_sta, n_src, chunk),
        out_shape=(
            jax.ShapeDtypeStruct((windows, cols), F32),
            jax.ShapeDtypeStruct((rows, cols, lanes), BF16),
            jax.ShapeDtypeStruct((w_rows, lanes), F32),
        ),
        in_specs=[vmem] * 9,
        out_specs=(vmem,) * 3,
        scratch_shapes=[
            pltpu.VMEM((2 * LAYERS, span_s, cols, lanes), BF16),
            pltpu.VMEM((2 * LAYERS, rows, span_r, lanes), BF16),
            pltpu.VMEM((LAYERS, rows, cols, 3 * lanes), BF16),
            pltpu.VMEM((rows, cols, 3 * lanes), BF16),
            pltpu.VMEM((LAYERS, nodes, lanes), F32),
            pltpu.VMEM((2, rows * J, span_s * J), BF16),
            pltpu.VMEM((2, G * cols, G * span_r), BF16),
            pltpu.VMEM((2, LAYERS, 3 * lanes, lanes), BF16),
            pltpu.VMEM((jw, nodes), BF16),
            pltpu.VMEM((nodes, jw), BF16),
            pltpu.VMEM((n_sta, 8, lanes), F32),
            pltpu.VMEM((w_rows, lanes), F32),
            pltpu.VMEM((n_sta, chunk, lanes), F32),
            pltpu.VMEM((n_src, chunk, lanes), F32),
            pltpu.VMEM((w_rows, lanes), F32),
            dma((2 * LAYERS, 4)),
            dma((2 * LAYERS, 4)),
            dma((n_sta,)),
            dma((n_sta,)),
            dma((n_sta,)),
            dma((n_sta,)),
            dma((n_src,)),
            dma((n_src,)),
            dma((n_sta,)),
            dma((n_sta,)),
        ],
        compiler_params=pltpu.CompilerParams(
            collective_id=0, has_side_effects=True, vmem_limit_bytes=48 * 1024 * 1024
        ),
    )(
        features,
        station_lists,
        station_counts.reshape(1, -1),
        source_lists,
        source_counts.reshape(1, -1),
        picks,
        targets,
        layer_weights,
        readout_vector.reshape(1, -1),
    )
    node_total = jnp.float32(rows * n_sta) * jnp.float32(cols * n_src)
    factor = 1.0 / jnp.sqrt(node_total)
    blocks = w_sum[: 3 * feature].reshape(3, feature, 2, feature).transpose(0, 2, 3, 1)
    w_total = jnp.stack(
        [jnp.concatenate([blocks[l], blocks[2, l : l + 1]], 0) for l in range(LAYERS)]
    )
    v_total = jnp.sum(w_sum[3 * feature].reshape(windows, feature), axis=0)
    return (lik, grad, w_total * factor, v_total * factor)


def solution(mesh):
    in_specs = (P("sta", "src", None), P(), P(), P(), P(), P(None, "sta"), P(None, "src"), P(), P())
    out_specs = (P(None, "src"), P("sta", "src", None), P(), P())
    body = functools.partial(shards, mesh.shape["sta"], mesh.shape["src"])
    return jax.shard_map(body, mesh=mesh, in_specs=in_specs, out_specs=out_specs, check_vma=False)
```

```python
import functools

import jax
import jax.numpy as jnp
import numpy as np
from jax import lax
from jax.experimental import pallas as pl
from jax.experimental.pallas import tpu as pltpu
from jax.sharding import PartitionSpec as P

LAYERS = 2
HW = 16
J = 16
G = 4
HALVES = 2
MESH = pl.DeviceIdType.MESH
F32, BF16 = jnp.float32, jnp.bfloat16


def iota(shape, dim):
    return lax.broadcasted_iota(jnp.int32, shape, dim)


def ones_where(cond):
    return jnp.where(cond, 1.0, 0.0).astype(BF16)


def dot(a, b):
    return lax.dot_general(a, b, (((1,), (0,)), ((), ())), preferred_element_type=F32)


def dot_nt(a, b):
    return lax.dot_general(a, b, (((1,), (1,)), ((), ())), preferred_element_type=F32)


def dot_tn(a, b):
    return lax.dot_general(a, b, (((0,), (0,)), ((), ())), preferred_element_type=F32)


def coefs(lists, count_row, base, span):
    total_rows = lists.shape[1]
    count = jnp.broadcast_to(count_row, (span, total_rows))
    place = iota((span, total_rows), 0) + base
    total = jnp.zeros((span, total_rows), F32)
    for k in range(lists.shape[0]):
        hit = (place == lists[k : k + 1]) & (count > float(k))
        total = total + jnp.where(hit, 1.0, 0.0)
    return (total / count).astype(BF16)


def kernel(
    n_sta,
    n_src,
    chunk,
    feat,
    slist,
    scnt,
    rlist,
    rcnt,
    picks,
    targets,
    weights,
    readout,
    lik_out,
    grad_out,
    w_out,
    hs,
    hr,
    x,
    xb,
    slope,
    ks,
    bd,
    wf,
    q,
    qt,
    lik_slots,
    w_local,
    sta_slots,
    src_slots,
    total,
    load_sem,
    halo_send,
    halo_recv,
    lik_send,
    lik_recv,
    a_send,
    a_recv,
    b_send,
    b_recv,
    c_send,
    c_recv,
):
    me_sta = lax.axis_index("sta")
    me_src = lax.axis_index("src")
    rows, cols, lanes = feat.shape
    feature = weights.shape[-1]
    windows = lanes // feature
    half = rows // HALVES
    span_s, span_r, span_h = rows + 2 * HW, cols + 2 * HW, half + 2 * HW
    nodes, part_nodes = rows * cols, half * cols
    all_sta, all_src = rows * n_sta, cols * n_src
    sta_first, src_first = me_sta * rows, me_src * cols

    def sta_peer(d):
        return lax.rem(me_sta + d, n_sta)

    def src_peer(d):
        return lax.rem(me_src + d, n_src)

    loads = [
        pltpu.make_async_copy(feat, hs.at[0, HW : HW + rows], load_sem.at[0]),
        pltpu.make_async_copy(feat, hr.at[0, :, HW : HW + cols], load_sem.at[1]),
        pltpu.make_async_copy(feat, x.at[0, :, :, 0:lanes], load_sem.at[2]),
    ]
    for copy in loads:
        copy.start()

    for e in range(2 * LAYERS):
        zero_s = jnp.zeros((HW, cols, lanes), BF16)
        zero_r = jnp.zeros((rows, HW, lanes), BF16)

        @pl.when(me_sta == 0)
        def _():
            hs[e, 0:HW] = zero_s

        @pl.when(me_sta == n_sta - 1)
        def _():
            hs[e, HW + rows :] = zero_s

        @pl.when(me_src == 0)
        def _():
            hr[e, :, 0:HW] = zero_r

        @pl.when(me_src == n_src - 1)
        def _():
            hr[e, :, HW + cols :] = zero_r

    barrier = pltpu.get_barrier_semaphore()
    for d in range(1, n_sta):
        pl.semaphore_signal(barrier, inc=1, device_id={"sta": sta_peer(d)}, device_id_type=MESH)
    for d in range(1, n_src):
        pl.semaphore_signal(barrier, inc=1, device_id={"src": src_peer(d)}, device_id_type=MESH)
    pl.semaphore_wait(barrier, n_sta + n_src - 2)

    def halo_copy(e, direction):
        h = (direction - 2) // 2
        own = slice(h * half, (h + 1) * half)
        if direction == 0:
            dst, device = hs.at[e, HW + rows :], {"sta": me_sta - 1}
            src = feat.at[0:HW] if e == 0 else hs.at[e, HW : 2 * HW]
        elif direction == 1:
            dst, device = hs.at[e, 0:HW], {"sta": me_sta + 1}
            src = feat.at[rows - HW :] if e == 0 else hs.at[e, rows : HW + rows]
        elif direction % 2 == 0:
            dst, device = hr.at[e, own, HW + cols :], {"src": me_src - 1}
            src = feat.at[own, 0:HW] if e == 0 else hr.at[e, own, HW : 2 * HW]
        else:
            dst, device = hr.at[e, own, 0:HW], {"src": me_src + 1}
            src = feat.at[own, cols - HW :] if e == 0 else hr.at[e, own, cols : HW + cols]
        return pltpu.make_async_remote_copy(
            src_ref=src,
            dst_ref=dst,
            send_sem=halo_send.at[e, direction],
            recv_sem=halo_recv.at[e, direction],
            device_id=device,
            device_id_type=MESH,
        )

    sides = [me_sta > 0, me_sta < n_sta - 1, me_src > 0, me_src < n_src - 1]

    def goes(direction):
        return sides[direction if direction < 2 else 2 + direction % 2]

    def comes(direction):
        return sides[1 - direction if direction < 2 else 3 - direction % 2]

    def halo_start(e, directions):
        for direction in directions:
            pl.when(goes(direction))(lambda: halo_copy(e, direction).start())

    def halo_wait(e, directions):
        for direction in directions:
            pl.when(comes(direction))(lambda: halo_copy(e, direction).wait_recv())

    def halo_drain(e):
        for direction in range(2 + 2 * HALVES):
            pl.when(goes(direction))(lambda: halo_copy(e, direction).wait_send())

    def halo_put(e, h, values):
        own = slice(h * half, (h + 1) * half)
        hr[e, own, HW : HW + cols] = values
        halo_start(e, (2 + 2 * h, 3 + 2 * h))
        hs[e, HW + h * half : HW + (h + 1) * half] = values
        halo_start(e, (h,))

    for h in range(HALVES):
        halo_start(0, (2 + 2 * h, 3 + 2 * h))
    halo_start(0, (0, 1))

    s_row, r_row = scnt[...].astype(F32), rcnt[...].astype(F32)
    s_lists, r_lists = slist[...], rlist[...]
    same_col = (iota((half * J, span_h * J), 0) % J) == (iota((half * J, span_h * J), 1) % J)
    same_grp = (iota((G * cols, G * span_r), 0) // cols) == (iota((G * cols, G * span_r), 1) // span_r)

    def put_mixes(way, left_s, cols_s, left_r, cols_r):
        left_s, left_r = left_s.astype(BF16), left_r.astype(BF16)
        for h in range(HALVES):
            right = cols_s[:, h * half * J : (h * half + span_h) * J]
            wide = dot(left_s[h * half * J : (h + 1) * half * J], right)
            ks[way, h] = jnp.where(same_col, wide, 0.0).astype(BF16)
        bd[way] = jnp.where(same_grp, dot(left_r, cols_r), 0.0).astype(BF16)

    def forward_mixes():
        fwd_s = coefs(s_lists, s_row, sta_first - HW, span_s)
        fwd_r = coefs(r_lists, r_row, src_first - HW, span_r)
        row_s = (rows * J, all_sta)
        row_r = (G * cols, all_src)
        put_mixes(
            0,
            dot_nt(ones_where(iota(row_s, 0) // J + sta_first == iota(row_s, 1)), fwd_s),
            ones_where((iota((span_s, span_s * J), 1) // J) == iota((span_s, span_s * J), 0)),
            dot_nt(ones_where(iota(row_r, 0) % cols + src_first == iota(row_r, 1)), fwd_r),
            ones_where((iota((span_r, G * span_r), 1) % span_r) == iota((span_r, G * span_r), 0)),
        )

    def backward_mixes():
        bwd_s = coefs(s_lists, s_row, sta_first, rows)
        bwd_r = coefs(r_lists, r_row, src_first, cols)
        col_s = (all_sta, span_s * J)
        col_r = (all_src, G * span_r)
        put_mixes(
            1,
            dot(ones_where((iota((rows * J, rows), 0) // J) == iota((rows * J, rows), 1)), bwd_s),
            ones_where(iota(col_s, 1) // J + (sta_first - HW) == iota(col_s, 0)),
            dot(ones_where((iota((G * cols, cols), 0) % cols) == iota((G * cols, cols), 1)), bwd_r),
            ones_where(iota(col_r, 1) % span_r + (src_first - HW) == iota(col_r, 0)),
        )

    spread = ones_where((iota((lanes, feature), 0) % feature) == iota((lanes, feature), 1))
    first_window = iota((feature, lanes), 1) < feature

    def put_weights():
        count = LAYERS * 3
        stack = weights[...].reshape(count * feature, feature)
        wide = dot_nt(stack, spread)
        double = jnp.concatenate([weights[n // 3, n % 3] for n in range(count) for _ in range(2)], axis=0)
        eye = ones_where(iota((feature, feature), 0) == iota((feature, feature), 1))
        turned = dot_nt(eye, double)
        for n in range(count):
            l, p = n // 3, n % 3
            for way, m in (
                (0, wide[n * feature : (n + 1) * feature]),
                (1, turned[:, n * lanes : (n + 1) * lanes]),
            ):
                top = slice(p * lanes, p * lanes + feature)
                low = slice(p * lanes + feature, (p + 1) * lanes)
                wf[way, l, top] = jnp.where(first_window, m, 0.0).astype(BF16)
                wf[way, l, low] = jnp.where(first_window, 0.0, m).astype(BF16)

    forward_mixes()
    put_weights()
    for copy in loads:
        copy.wait()

    def mix_sta(way, e, h, out):
        own = slice(h * half, (h + 1) * half)
        for j in range(0, cols, J):
            part = hs[e, h * half : h * half + span_h, j : j + J, :].reshape(span_h * J, lanes)
            mixed = dot(ks[way, h], part).astype(BF16)
            out[own, j : j + J, lanes : 2 * lanes] = mixed.reshape(half, J, lanes)

    def mix_src(way, e, h, out):
        for g in range(h * half, (h + 1) * half, G):
            part = hr[e, g : g + G].reshape(G * span_r, lanes)
            mixed = dot(bd[way], part).astype(BF16)
            out[g : g + G, :, 2 * lanes :] = mixed.reshape(G, cols, lanes)

    wide_readout = dot_nt(readout[...], spread)
    jw = windows * cols
    node_own = iota((jw, lanes), 0)
    win_mask = (node_own // cols) == (iota((jw, lanes), 1) // feature)
    diag = (node_own % cols) == iota((jw, lanes), 1)

    def to_column(row_of):
        wide = jnp.concatenate(
            [jnp.broadcast_to(row_of(w), (cols, lanes)) for w in range(windows)], axis=0
        )
        return jnp.sum(jnp.where(diag, wide, 0.0), axis=1, keepdims=True)

    picked = picks[...].astype(F32)
    for l in range(LAYERS):
        if l == 1:
            backward_mixes()
            wide_picks = jnp.concatenate(
                [jnp.broadcast_to(picked[w : w + 1], (cols, rows)) for w in range(windows)], axis=0
            ).astype(BF16)
            sel = ones_where((iota((nodes, rows), 0) // cols) == iota((nodes, rows), 1))
            at_q = (iota((jw, nodes), 0) % cols) == (iota((jw, nodes), 1) % cols)
            q[...] = jnp.where(at_q, dot_nt(wide_picks, sel), 0.0).astype(BF16)
            at_t = (iota((nodes, jw), 0) % cols) == (iota((nodes, jw), 1) % cols)
            qt[...] = jnp.where(at_t, dot_nt(sel, wide_picks), 0.0).astype(BF16)
        for h in range(HALVES):
            own = slice(h * half, (h + 1) * half)
            halo_wait(l, (1 - h,))
            mix_sta(0, l, h, x.at[l])
            halo_wait(l, (2 + 2 * h, 3 + 2 * h))
            mix_src(0, l, h, x.at[l])
            z = dot(x[l, own].reshape(part_nodes, 3 * lanes), wf[0, l])
            squashed = jnp.tanh(z)
            slope[l, h] = 1.0 - squashed * squashed
            before = x[l, own, :, 0:lanes].astype(F32)
            states = (before + squashed.reshape(half, cols, lanes)).astype(BF16)
            if l + 1 < LAYERS:
                halo_put(l + 1, h, states)
                x[l + 1, own, :, 0:lanes] = states
            else:
                xb[own, :, 0:lanes] = states

    heap = dot(q[...], xb[:, :, 0:lanes].reshape(nodes, lanes))
    score = jnp.sum(jnp.where(win_mask, heap * wide_readout, 0.0), axis=1, keepdims=True)
    flat = jnp.where(diag, score, 0.0)
    tile_row = iota((8, lanes), 0)
    tile = jnp.zeros((8, lanes), F32)
    for w in range(windows):
        part = jnp.sum(flat[w * cols : (w + 1) * cols], axis=0, keepdims=True)
        tile = jnp.where(tile_row == w, part, tile)
        count = jnp.sum(picked[w : w + 1], axis=1, keepdims=True)
        tile = jnp.where(tile_row == windows + w, count, tile)
    lik_slots[me_sta] = tile
    sends = []
    for d in range(1, n_sta):
        sends.append(
            pltpu.make_async_remote_copy(
                src_ref=lik_slots.at[me_sta],
                dst_ref=lik_slots.at[me_sta],
                send_sem=lik_send.at[d],
                recv_sem=lik_recv.at[d],
                device_id={"sta": sta_peer(d)},
                device_id_type=MESH,
            )
        )
        sends[-1].start()
    for copy in sends:
        copy.wait_recv()
    summed = lik_slots[0]
    for s in range(1, n_sta):
        summed = summed + lik_slots[s]
    root = jnp.sqrt(jnp.maximum(summed[windows : 2 * windows], 1.0))
    lik = summed[0:windows] / root
    lik_out[...] = lik[:, :cols]
    sig = jax.nn.sigmoid(lik)
    sig_col = to_column(lambda w: sig[w : w + 1])
    want = jnp.concatenate(
        [jnp.broadcast_to(targets[w : w + 1, :], (cols, cols)) for w in range(windows)], axis=0
    )
    diag_cols = (iota((jw, cols), 0) % cols) == iota((jw, cols), 1)
    want_col = jnp.sum(jnp.where(diag_cols, want, 0.0), axis=1, keepdims=True)
    err = (sig_col - want_col).astype(BF16).astype(F32)
    err_wide = jnp.where(win_mask, err, 0.0)
    v_row = jnp.sum(err_wide * heap, axis=0, keepdims=True)

    def put_delta(l, h, grad):
        delta = (grad * slope[l, h]).astype(BF16).reshape(half, cols, lanes)
        halo_put(2 * LAYERS - 1 - l, h, delta)
        xb[h * half : (h + 1) * half, :, 0:lanes] = delta

    grads = []
    for h in range(HALVES):
        spot = slice(h * part_nodes, (h + 1) * part_nodes)
        grads.append(dot(qt[spot], err_wide.astype(BF16)) * wide_readout)
        put_delta(LAYERS - 1, h, grads[h])

    def weight_sums(l):
        w_t = dot_tn(xb[:, :, 0:lanes].reshape(nodes, lanes), x[l].reshape(nodes, 3 * lanes))
        folded = []
        for p in range(3):
            both = jnp.where(
                first_window,
                w_t[0:feature, p * lanes : (p + 1) * lanes],
                w_t[feature:, p * lanes : (p + 1) * lanes],
            )
            folded.append(both + pltpu.roll(both, feature, 1))
        base = l * feature
        w_local[base : base + feature] = jnp.where(first_window, folded[0], folded[1])
        return folded[2]

    def chunk_of(ref, s):
        return ref.at[pl.ds(pl.multiple_of(s * chunk, 8), chunk)]

    first, second, third = [], [], []
    for l in reversed(range(LAYERS)):
        e = 2 * LAYERS - 1 - l
        if l == 1:
            kept = weight_sums(l)
        else:
            w_local[2 * feature : 3 * feature] = jnp.where(first_window, weight_sums(l), kept)
            w_local[3 * feature :] = jnp.broadcast_to(v_row, (w_local.shape[0] - 3 * feature, lanes))
            for d in range(1, n_sta):
                first.append(
                    pltpu.make_async_remote_copy(
                        src_ref=chunk_of(w_local, sta_peer(d)),
                        dst_ref=sta_slots.at[me_sta],
                        send_sem=a_send.at[d],
                        recv_sem=a_recv.at[d],
                        device_id={"sta": sta_peer(d)},
                        device_id_type=MESH,
                    )
                )
                first[-1].start()
            sta_slots[me_sta] = chunk_of(w_local, me_sta)[...]
        for h in range(HALVES):
            own = slice(h * half, (h + 1) * half)
            halo_wait(e, (1 - h,))
            mix_sta(1, e, h, xb)
            if l == 0 and h == 0:
                for copy in first:
                    copy.wait_recv()
                some = sta_slots[0]
                for s in range(1, n_sta):
                    some = some + sta_slots[s]
                src_slots[me_src] = some
                for d in range(1, n_src):
                    second.append(
                        pltpu.make_async_remote_copy(
                            src_ref=src_slots.at[me_src],
                            dst_ref=src_slots.at[me_src],
                            send_sem=b_send.at[d],
                            recv_sem=b_recv.at[d],
                            device_id={"src": src_peer(d)},
                            device_id_type=MESH,
                        )
                    )
                    second[-1].start()
            halo_wait(e, (2 + 2 * h, 3 + 2 * h))
            mix_src(1, e, h, xb)
            grad = grads[h] + dot(xb[own].reshape(part_nodes, 3 * lanes), wf[1, l])
            if l > 0:
                grads[h] = grad
                put_delta(l - 1, h, grad)
            else:
                grad_out[own] = grad.reshape(half, cols, lanes).astype(BF16)

    for copy in second:
        copy.wait_recv()
    some = src_slots[0]
    for s in range(1, n_src):
        some = some + src_slots[s]
    chunk_of(total, me_sta)[...] = some
    for d in range(1, n_sta):
        third.append(
            pltpu.make_async_remote_copy(
                src_ref=chunk_of(total, me_sta),
                dst_ref=chunk_of(total, me_sta),
                send_sem=c_send.at[d],
                recv_sem=c_recv.at[d],
                device_id={"sta": sta_peer(d)},
                device_id_type=MESH,
            )
        )
        third[-1].start()
    for e in range(2 * LAYERS):
        halo_drain(e)
    for copy in sends + first + second:
        copy.wait_send()
    for copy in third:
        copy.wait_recv()
    w_out[...] = total[...]
    for copy in third:
        copy.wait_send()


def finish(factor, windows, lik, grad, w_sum, lik_out, grad_out, w_out, v_out):
    lik_out[...] = lik[...]
    grad_out[...] = grad[...]
    feature = w_out.shape[-1]
    for t in range(3):
        turned = jnp.transpose(w_sum[t * feature : (t + 1) * feature] * factor)
        for n in range(2):
            l, p = (t, n) if t < 2 else (n, 2)
            w_out[l, p] = turned[n * feature : (n + 1) * feature]
    row = w_sum[3 * feature : 3 * feature + 1] * factor
    v_out[...] = (row + pltpu.roll(row, feature, 1))[:, :feature]


def shards(
    n_sta,
    n_src,
    features,
    station_lists,
    station_counts,
    source_lists,
    source_counts,
    picks,
    targets,
    layer_weights,
    readout_vector,
):
    rows, cols, lanes = features.shape
    feature = layer_weights.shape[-1]
    windows = lanes // feature
    nodes = rows * cols
    half = rows // HALVES
    span_s, span_r = rows + 2 * HW, cols + 2 * HW
    chunk = -(-(3 * feature + 1) // (8 * n_sta)) * 8
    w_rows = chunk * n_sta
    jw = windows * cols
    dma = pltpu.SemaphoreType.DMA
    vmem = pl.BlockSpec(memory_space=pltpu.VMEM)
    lik, grad, w_sum = pl.pallas_call(
        functools.partial(kernel, n_sta, n_src, chunk),
        out_shape=(
            jax.ShapeDtypeStruct((windows, cols), F32),
            jax.ShapeDtypeStruct((rows, cols, lanes), BF16),
            jax.ShapeDtypeStruct((w_rows, lanes), F32),
        ),
        in_specs=[pl.BlockSpec(memory_space=pl.ANY)] + [vmem] * 8,
        out_specs=(vmem,) * 3,
        scratch_shapes=[
            pltpu.VMEM((2 * LAYERS, span_s, cols, lanes), BF16),
            pltpu.VMEM((2 * LAYERS, rows, span_r, lanes), BF16),
            pltpu.VMEM((LAYERS, rows, cols, 3 * lanes), BF16),
            pltpu.VMEM((rows, cols, 3 * lanes), BF16),
            pltpu.VMEM((LAYERS, HALVES, nodes // HALVES, lanes), F32),
            pltpu.VMEM((2, HALVES, half * J, (half + 2 * HW) * J), BF16),
            pltpu.VMEM((2, G * cols, G * span_r), BF16),
            pltpu.VMEM((2, LAYERS, 3 * lanes, lanes), BF16),
            pltpu.VMEM((jw, nodes), BF16),
            pltpu.VMEM((nodes, jw), BF16),
            pltpu.VMEM((n_sta, 8, lanes), F32),
            pltpu.VMEM((w_rows, lanes), F32),
            pltpu.VMEM((n_sta, chunk, lanes), F32),
            pltpu.VMEM((n_src, chunk, lanes), F32),
            pltpu.VMEM((w_rows, lanes), F32),
            dma((3,)),
            dma((2 * LAYERS, 2 + 2 * HALVES)),
            dma((2 * LAYERS, 2 + 2 * HALVES)),
            dma((n_sta,)),
            dma((n_sta,)),
            dma((n_sta,)),
            dma((n_sta,)),
            dma((n_src,)),
            dma((n_src,)),
            dma((n_sta,)),
            dma((n_sta,)),
        ],
        compiler_params=pltpu.CompilerParams(
            collective_id=0, has_side_effects=True, vmem_limit_bytes=48 * 1024 * 1024
        ),
    )(
        features,
        station_lists.T,
        station_counts.reshape(1, -1),
        source_lists.T,
        source_counts.reshape(1, -1),
        picks,
        targets,
        layer_weights,
        readout_vector.reshape(1, -1),
    )
    factor = float(1.0 / np.sqrt(np.float32(rows * n_sta * cols * n_src)))
    lik, grad, w_total, v_total = pl.pallas_call(
        functools.partial(finish, factor, windows),
        out_shape=(
            jax.ShapeDtypeStruct(lik.shape, F32),
            jax.ShapeDtypeStruct(grad.shape, BF16),
            jax.ShapeDtypeStruct(layer_weights.shape, F32),
            jax.ShapeDtypeStruct((1, feature), F32),
        ),
        in_specs=[vmem] * 3,
        out_specs=(vmem,) * 4,
    )(lik, grad, w_sum)
    return (lik, grad, w_total, v_total.reshape(feature))


def solution(mesh):
    in_specs = (P("sta", "src", None), P(), P(), P(), P(), P(None, "sta"), P(None, "src"), P(), P())
    out_specs = (P(None, "src"), P("sta", "src", None), P(), P())
    body = functools.partial(shards, mesh.shape["sta"], mesh.shape["src"])
    return jax.shard_map(body, mesh=mesh, in_specs=in_specs, out_specs=out_specs, check_vma=False)
```

```python
import functools

import jax
import jax.numpy as jnp
import numpy as np
from jax import lax
from jax.experimental import pallas as pl
from jax.experimental.pallas import tpu as pltpu
from jax.sharding import PartitionSpec as P

LAYERS = 2
HW = 16
J = 16
G = 4
HALVES = 2
VMEM = 60 * 1024 * 1024
MESH = pl.DeviceIdType.MESH
F32, BF16 = jnp.float32, jnp.bfloat16


def iota(shape, dim):
    return lax.broadcasted_iota(jnp.int32, shape, dim)


def ones_where(cond):
    return jnp.where(cond, 1.0, 0.0).astype(BF16)


def over(value, size):
    return lax.shift_right_logical(value, jnp.full(value.shape, size.bit_length() - 1, jnp.int32))


def within(value, size):
    return value & (size - 1)


def dot(a, b):
    return lax.dot_general(a, b, (((1,), (0,)), ((), ())), preferred_element_type=F32)


def dot_nt(a, b):
    return lax.dot_general(a, b, (((1,), (1,)), ((), ())), preferred_element_type=F32)


def dot_tn(a, b):
    return lax.dot_general(a, b, (((0,), (0,)), ((), ())), preferred_element_type=F32)


def coefs(lists, count_row, base, span):
    total_rows = lists.shape[1]
    count = jnp.broadcast_to(count_row, (span, total_rows))
    place = iota((span, total_rows), 0) + base
    total = jnp.zeros((span, total_rows), F32)
    for k in range(lists.shape[0]):
        hit = (place == lists[k : k + 1]) & (count > float(k))
        total = total + jnp.where(hit, 1.0, 0.0)
    return (total * (1.0 / count_row)).astype(BF16)


def kernel(
    n_sta,
    n_src,
    chunk,
    feat,
    slist_hbm,
    scnt_hbm,
    rlist_hbm,
    rcnt_hbm,
    picks_hbm,
    targets_hbm,
    weights_hbm,
    readout_hbm,
    lik_hbm,
    grad_hbm,
    w_hbm,
    slist,
    scnt,
    rlist,
    rcnt,
    picks,
    targets,
    weights,
    readout,
    lik_out,
    grad_out,
    hs,
    hr,
    x,
    xb,
    slope,
    ks,
    bd,
    wf,
    q,
    qt,
    lik_slots,
    w_local,
    sta_slots,
    src_slots,
    total,
    load_sem,
    out_sem,
    halo_send,
    halo_recv,
    lik_send,
    lik_recv,
    a_send,
    a_recv,
    b_send,
    b_recv,
    c_send,
    c_recv,
):
    me_sta = lax.axis_index("sta")
    me_src = lax.axis_index("src")
    rows, cols, lanes = feat.shape
    feature = weights.shape[-1]
    windows = lanes // feature
    half = rows // HALVES
    span_s, span_r, span_h = rows + 2 * HW, cols + 2 * HW, half + 2 * HW
    nodes, part_nodes = rows * cols, half * cols
    all_sta, all_src = rows * n_sta, cols * n_src
    sta_first, src_first = me_sta * rows, me_src * cols

    def sta_peer(d):
        return lax.rem(me_sta + d, n_sta)

    def src_peer(d):
        return lax.rem(me_src + d, n_src)

    loads = [
        pltpu.make_async_copy(feat, hs.at[0, HW : HW + rows], load_sem.at[0]),
        pltpu.make_async_copy(feat, hr.at[0, :, HW : HW + cols], load_sem.at[1]),
        pltpu.make_async_copy(feat, x.at[0, :, :, 0:lanes], load_sem.at[2]),
    ]
    pairs = [
        (slist_hbm, slist),
        (scnt_hbm, scnt),
        (rlist_hbm, rlist),
        (rcnt_hbm, rcnt),
        (picks_hbm, picks),
        (targets_hbm, targets),
        (weights_hbm, weights),
        (readout_hbm, readout),
    ]
    small = [pltpu.make_async_copy(a, b, load_sem.at[3 + n]) for n, (a, b) in enumerate(pairs)]
    for copy in small + loads:
        copy.start()

    for e in range(2 * LAYERS):
        zero_s = jnp.zeros((HW, cols, lanes), BF16)
        zero_r = jnp.zeros((rows, HW, lanes), BF16)

        @pl.when(me_sta == 0)
        def _():
            hs[e, 0:HW] = zero_s

        @pl.when(me_sta == n_sta - 1)
        def _():
            hs[e, HW + rows :] = zero_s

        @pl.when(me_src == 0)
        def _():
            hr[e, :, 0:HW] = zero_r

        @pl.when(me_src == n_src - 1)
        def _():
            hr[e, :, HW + cols :] = zero_r

    barrier = pltpu.get_barrier_semaphore()
    for d in range(1, n_sta):
        pl.semaphore_signal(barrier, inc=1, device_id={"sta": sta_peer(d)}, device_id_type=MESH)
    for d in range(1, n_src):
        pl.semaphore_signal(barrier, inc=1, device_id={"src": src_peer(d)}, device_id_type=MESH)

    for copy in small:
        copy.wait()
    s_row, r_row = scnt[...].astype(F32), rcnt[...].astype(F32)
    s_lists, r_lists = slist[...], rlist[...]
    same_col = within(iota((half * J, span_h * J), 0), J) == within(iota((half * J, span_h * J), 1), J)
    same_grp = over(iota((G * cols, G * span_r), 0), cols) == over(iota((G * cols, G * span_r), 1), span_r)

    def put_mixes(way, left_s, cols_s, left_r, cols_r):
        left_s, left_r = left_s.astype(BF16), left_r.astype(BF16)
        for h in range(HALVES):
            right = cols_s[:, h * half * J : (h * half + span_h) * J]
            wide = dot(left_s[h * half * J : (h + 1) * half * J], right)
            ks[way, h] = jnp.where(same_col, wide, 0.0).astype(BF16)
        bd[way] = jnp.where(same_grp, dot(left_r, cols_r), 0.0).astype(BF16)

    def forward_mixes():
        fwd_s = coefs(s_lists, s_row, sta_first - HW, span_s)
        fwd_r = coefs(r_lists, r_row, src_first - HW, span_r)
        row_s = (rows * J, all_sta)
        row_r = (G * cols, all_src)
        put_mixes(
            0,
            dot_nt(ones_where(over(iota(row_s, 0), J) + sta_first == iota(row_s, 1)), fwd_s),
            ones_where(over(iota((span_s, span_s * J), 1), J) == iota((span_s, span_s * J), 0)),
            dot_nt(ones_where(within(iota(row_r, 0), cols) + src_first == iota(row_r, 1)), fwd_r),
            ones_where(within(iota((span_r, G * span_r), 1), span_r) == iota((span_r, G * span_r), 0)),
        )

    forward_mixes()
    pl.semaphore_wait(barrier, n_sta + n_src - 2)

    def halo_copy(e, direction):
        h = (direction - 2) // 2
        own = slice(h * half, (h + 1) * half)
        if direction == 0:
            dst, device = hs.at[e, HW + rows :], {"sta": me_sta - 1}
            src = feat.at[0:HW] if e == 0 else hs.at[e, HW : 2 * HW]
        elif direction == 1:
            dst, device = hs.at[e, 0:HW], {"sta": me_sta + 1}
            src = feat.at[rows - HW :] if e == 0 else hs.at[e, rows : HW + rows]
        elif direction % 2 == 0:
            dst, device = hr.at[e, own, HW + cols :], {"src": me_src - 1}
            src = feat.at[own, 0:HW] if e == 0 else hr.at[e, own, HW : 2 * HW]
        else:
            dst, device = hr.at[e, own, 0:HW], {"src": me_src + 1}
            src = feat.at[own, cols - HW :] if e == 0 else hr.at[e, own, cols : HW + cols]
        return pltpu.make_async_remote_copy(
            src_ref=src,
            dst_ref=dst,
            send_sem=halo_send.at[e, direction],
            recv_sem=halo_recv.at[e, direction],
            device_id=device,
            device_id_type=MESH,
        )

    sides = [me_sta > 0, me_sta < n_sta - 1, me_src > 0, me_src < n_src - 1]

    def goes(direction):
        return sides[direction if direction < 2 else 2 + direction % 2]

    def comes(direction):
        return sides[1 - direction if direction < 2 else 3 - direction % 2]

    def halo_start(e, directions):
        for direction in directions:
            pl.when(goes(direction))(lambda: halo_copy(e, direction).start())

    def halo_wait(e, directions):
        for direction in directions:
            pl.when(comes(direction))(lambda: halo_copy(e, direction).wait_recv())

    def halo_drain(e):
        for direction in range(2 + 2 * HALVES):
            pl.when(goes(direction))(lambda: halo_copy(e, direction).wait_send())

    def halo_put(e, h, values):
        own = slice(h * half, (h + 1) * half)
        hr[e, own, HW : HW + cols] = values
        halo_start(e, (2 + 2 * h, 3 + 2 * h))
        hs[e, HW + h * half : HW + (h + 1) * half] = values
        halo_start(e, (h,))

    for h in range(HALVES):
        halo_start(0, (2 + 2 * h, 3 + 2 * h))
    halo_start(0, (0, 1))

    def backward_mixes():
        bwd_s = coefs(s_lists, s_row, sta_first, rows)
        bwd_r = coefs(r_lists, r_row, src_first, cols)
        col_s = (all_sta, span_s * J)
        col_r = (all_src, G * span_r)
        put_mixes(
            1,
            dot(ones_where(over(iota((rows * J, rows), 0), J) == iota((rows * J, rows), 1)), bwd_s),
            ones_where(over(iota(col_s, 1), J) + (sta_first - HW) == iota(col_s, 0)),
            dot(ones_where(within(iota((G * cols, cols), 0), cols) == iota((G * cols, cols), 1)), bwd_r),
            ones_where(within(iota(col_r, 1), span_r) + (src_first - HW) == iota(col_r, 0)),
        )

    spread = ones_where(within(iota((lanes, feature), 0), feature) == iota((lanes, feature), 1))
    first_window = iota((feature, lanes), 1) < feature

    def put_weights():
        count = LAYERS * 3
        stack = weights[...].reshape(count * feature, feature)
        wide = dot_nt(stack, spread)
        double = jnp.concatenate([weights[n // 3, n % 3] for n in range(count) for _ in range(2)], axis=0)
        eye = ones_where(iota((feature, feature), 0) == iota((feature, feature), 1))
        turned = dot_nt(eye, double)
        for n in range(count):
            l, p = n // 3, n % 3
            for way, m in (
                (0, wide[n * feature : (n + 1) * feature]),
                (1, turned[:, n * lanes : (n + 1) * lanes]),
            ):
                top = slice(p * lanes, p * lanes + feature)
                low = slice(p * lanes + feature, (p + 1) * lanes)
                wf[way, l, top] = jnp.where(first_window, m, 0.0).astype(BF16)
                wf[way, l, low] = jnp.where(first_window, 0.0, m).astype(BF16)

    put_weights()
    for copy in loads:
        copy.wait()

    def mix_sta(way, e, h, out):
        own = slice(h * half, (h + 1) * half)
        for j in range(0, cols, J):
            part = hs[e, h * half : h * half + span_h, j : j + J, :].reshape(span_h * J, lanes)
            mixed = dot(ks[way, h], part).astype(BF16)
            out[own, j : j + J, lanes : 2 * lanes] = mixed.reshape(half, J, lanes)

    def mix_src(way, e, h, out):
        for g in range(h * half, (h + 1) * half, G):
            part = hr[e, g : g + G].reshape(G * span_r, lanes)
            mixed = dot(bd[way], part).astype(BF16)
            out[g : g + G, :, 2 * lanes :] = mixed.reshape(G, cols, lanes)

    wide_readout = dot_nt(readout[...], spread)
    jw = windows * cols
    node_own = iota((jw, lanes), 0)
    win_mask = over(node_own, cols) == over(iota((jw, lanes), 1), feature)
    diag = within(node_own, cols) == iota((jw, lanes), 1)

    def to_column(row_of):
        wide = jnp.concatenate(
            [jnp.broadcast_to(row_of(w), (cols, lanes)) for w in range(windows)], axis=0
        )
        return jnp.sum(jnp.where(diag, wide, 0.0), axis=1, keepdims=True)

    picked = picks[...].astype(F32)
    for l in range(LAYERS):
        if l == 1:
            backward_mixes()
            wide_picks = jnp.concatenate(
                [jnp.broadcast_to(picked[w : w + 1], (cols, rows)) for w in range(windows)], axis=0
            ).astype(BF16)
            sel = ones_where(over(iota((nodes, rows), 0), cols) == iota((nodes, rows), 1))
            at_q = within(iota((jw, nodes), 0), cols) == within(iota((jw, nodes), 1), cols)
            q[...] = jnp.where(at_q, dot_nt(wide_picks, sel), 0.0).astype(BF16)
            at_t = within(iota((nodes, jw), 0), cols) == within(iota((nodes, jw), 1), cols)
            qt[...] = jnp.where(at_t, dot_nt(sel, wide_picks), 0.0).astype(BF16)
        for h in range(HALVES):
            own = slice(h * half, (h + 1) * half)
            halo_wait(l, (1 - h,))
            mix_sta(0, l, h, x.at[l])
            z = dot(x[l, own, :, 0 : 2 * lanes].reshape(part_nodes, 2 * lanes), wf[0, l, 0 : 2 * lanes])
            halo_wait(l, (2 + 2 * h, 3 + 2 * h))
            mix_src(0, l, h, x.at[l])
            z = z + dot(x[l, own, :, 2 * lanes :].reshape(part_nodes, lanes), wf[0, l, 2 * lanes :])
            squashed = jnp.tanh(z)
            slope[l, h] = 1.0 - squashed * squashed
            before = x[l, own, :, 0:lanes].astype(F32)
            states = (before + squashed.reshape(half, cols, lanes)).astype(BF16)
            if l + 1 < LAYERS:
                halo_put(l + 1, h, states)
                x[l + 1, own, :, 0:lanes] = states
            else:
                xb[own, :, 0:lanes] = states

    heap = dot(q[...], xb[:, :, 0:lanes].reshape(nodes, lanes))
    score = jnp.sum(jnp.where(win_mask, heap * wide_readout, 0.0), axis=1, keepdims=True)
    flat = jnp.where(diag, score, 0.0)
    tile_row = iota((8, lanes), 0)
    tile = jnp.zeros((8, lanes), F32)
    for w in range(windows):
        part = jnp.sum(flat[w * cols : (w + 1) * cols], axis=0, keepdims=True)
        tile = jnp.where(tile_row == w, part, tile)
        count = jnp.sum(picked[w : w + 1], axis=1, keepdims=True)
        tile = jnp.where(tile_row == windows + w, count, tile)
    lik_slots[me_sta] = tile
    sends = []
    for d in range(1, n_sta):
        sends.append(
            pltpu.make_async_remote_copy(
                src_ref=lik_slots.at[me_sta],
                dst_ref=lik_slots.at[me_sta],
                send_sem=lik_send.at[d],
                recv_sem=lik_recv.at[d],
                device_id={"sta": sta_peer(d)},
                device_id_type=MESH,
            )
        )
        sends[-1].start()
    for copy in sends:
        copy.wait_recv()
    summed = lik_slots[0]
    for s in range(1, n_sta):
        summed = summed + lik_slots[s]
    root = jnp.sqrt(jnp.maximum(summed[windows : 2 * windows], 1.0))
    lik = summed[0:windows] / root
    lik_out[...] = lik[:, :cols]
    outs = [pltpu.make_async_copy(lik_out, lik_hbm, out_sem.at[HALVES])]
    outs[0].start()
    sig = jax.nn.sigmoid(lik)
    sig_col = to_column(lambda w: sig[w : w + 1])
    want = jnp.concatenate(
        [jnp.broadcast_to(targets[w : w + 1, :], (cols, cols)) for w in range(windows)], axis=0
    )
    diag_cols = within(iota((jw, cols), 0), cols) == iota((jw, cols), 1)
    want_col = jnp.sum(jnp.where(diag_cols, want, 0.0), axis=1, keepdims=True)
    err = (sig_col - want_col).astype(BF16).astype(F32)
    err_wide = jnp.where(win_mask, err, 0.0)
    v_row = jnp.sum(err_wide * heap, axis=0, keepdims=True)

    def put_delta(l, h, grad):
        delta = (grad * slope[l, h]).astype(BF16).reshape(half, cols, lanes)
        halo_put(2 * LAYERS - 1 - l, h, delta)
        xb[h * half : (h + 1) * half, :, 0:lanes] = delta

    grads = []
    for h in range(HALVES):
        spot = slice(h * part_nodes, (h + 1) * part_nodes)
        grads.append(dot(qt[spot], err_wide.astype(BF16)) * wide_readout)
        put_delta(LAYERS - 1, h, grads[h])

    def weight_sums(l):
        w_t = dot_tn(xb[:, :, 0:lanes].reshape(nodes, lanes), x[l].reshape(nodes, 3 * lanes))
        folded = []
        for p in range(3):
            both = jnp.where(
                first_window,
                w_t[0:feature, p * lanes : (p + 1) * lanes],
                w_t[feature:, p * lanes : (p + 1) * lanes],
            )
            folded.append(both + pltpu.roll(both, feature, 1))
        base = l * feature
        w_local[base : base + feature] = jnp.where(first_window, folded[0], folded[1])
        return folded[2]

    def chunk_of(ref, s):
        return ref.at[pl.ds(pl.multiple_of(s * chunk, 8), chunk)]

    first, second, third = [], [], []
    for l in reversed(range(LAYERS)):
        e = 2 * LAYERS - 1 - l
        if l == 1:
            kept = weight_sums(l)
        else:
            w_local[2 * feature : 3 * feature] = jnp.where(first_window, weight_sums(l), kept)
            w_local[3 * feature :] = jnp.broadcast_to(v_row, (w_local.shape[0] - 3 * feature, lanes))
            for d in range(1, n_sta):
                first.append(
                    pltpu.make_async_remote_copy(
                        src_ref=chunk_of(w_local, sta_peer(d)),
                        dst_ref=sta_slots.at[me_sta],
                        send_sem=a_send.at[d],
                        recv_sem=a_recv.at[d],
                        device_id={"sta": sta_peer(d)},
                        device_id_type=MESH,
                    )
                )
                first[-1].start()
            sta_slots[me_sta] = chunk_of(w_local, me_sta)[...]
        for h in range(HALVES):
            own = slice(h * half, (h + 1) * half)
            halo_wait(e, (1 - h,))
            mix_sta(1, e, h, xb)
            if l == 0 and h == 0:
                for copy in first:
                    copy.wait_recv()
                some = sta_slots[0]
                for s in range(1, n_sta):
                    some = some + sta_slots[s]
                src_slots[me_src] = some
                for d in range(1, n_src):
                    second.append(
                        pltpu.make_async_remote_copy(
                            src_ref=src_slots.at[me_src],
                            dst_ref=src_slots.at[me_src],
                            send_sem=b_send.at[d],
                            recv_sem=b_recv.at[d],
                            device_id={"src": src_peer(d)},
                            device_id_type=MESH,
                        )
                    )
                    second[-1].start()
            early = xb[own, :, 0 : 2 * lanes].reshape(part_nodes, 2 * lanes)
            grad = grads[h] + dot(early, wf[1, l, 0 : 2 * lanes])
            halo_wait(e, (2 + 2 * h, 3 + 2 * h))
            mix_src(1, e, h, xb)
            late = xb[own, :, 2 * lanes :].reshape(part_nodes, lanes)
            grad = grad + dot(late, wf[1, l, 2 * lanes :])
            if l > 0:
                grads[h] = grad
                put_delta(l - 1, h, grad)
            else:
                grad_out[own] = grad.reshape(half, cols, lanes).astype(BF16)
                outs.append(pltpu.make_async_copy(grad_out.at[own], grad_hbm.at[own], out_sem.at[h]))
                outs[-1].start()

    for copy in second:
        copy.wait_recv()
    some = src_slots[0]
    for s in range(1, n_src):
        some = some + src_slots[s]
    chunk_of(total, me_sta)[...] = some
    for d in range(1, n_sta):
        third.append(
            pltpu.make_async_remote_copy(
                src_ref=chunk_of(total, me_sta),
                dst_ref=chunk_of(total, me_sta),
                send_sem=c_send.at[d],
                recv_sem=c_recv.at[d],
                device_id={"sta": sta_peer(d)},
                device_id_type=MESH,
            )
        )
        third[-1].start()
    for e in range(2 * LAYERS):
        halo_drain(e)
    for copy in sends + first + second:
        copy.wait_send()
    for copy in third:
        copy.wait_recv()
    outs.append(pltpu.make_async_copy(total, w_hbm, out_sem.at[HALVES + 1]))
    outs[-1].start()
    for copy in third:
        copy.wait_send()
    for copy in outs:
        copy.wait()


def finish(factor, lik, grad, w_sum, lik_out, grad_out, w_out, v_out, sums, sems):
    load = pltpu.make_async_copy(w_sum, sums, sems.at[0])
    pass_grad = pltpu.make_async_copy(grad, grad_out, sems.at[1])
    pass_lik = pltpu.make_async_copy(lik, lik_out, sems.at[2])
    load.start()
    pass_grad.start()
    pass_lik.start()
    load.wait()
    feature = w_out.shape[-1]
    for t in range(3):
        turned = jnp.transpose(sums[t * feature : (t + 1) * feature] * factor)
        for n in range(2):
            l, p = (t, n) if t < 2 else (n, 2)
            w_out[l, p] = turned[n * feature : (n + 1) * feature]
    row = sums[3 * feature : 3 * feature + 1] * factor
    v_out[...] = (row + pltpu.roll(row, feature, 1))[:, :feature]
    pass_grad.wait()
    pass_lik.wait()


def shards(
    n_sta,
    n_src,
    features,
    station_lists,
    station_counts,
    source_lists,
    source_counts,
    picks,
    targets,
    layer_weights,
    readout_vector,
):
    rows, cols, lanes = features.shape
    feature = layer_weights.shape[-1]
    windows = lanes // feature
    nodes = rows * cols
    half = rows // HALVES
    span_s, span_r = rows + 2 * HW, cols + 2 * HW
    chunk = -(-(3 * feature + 1) // (8 * n_sta)) * 8
    w_rows = chunk * n_sta
    jw = windows * cols
    dma = pltpu.SemaphoreType.DMA
    hbm = pl.BlockSpec(memory_space=pl.ANY)
    vmem = pl.BlockSpec(memory_space=pltpu.VMEM)
    operands = (
        features,
        station_lists.T,
        station_counts.reshape(1, -1),
        source_lists.T,
        source_counts.reshape(1, -1),
        picks,
        targets,
        layer_weights,
        readout_vector.reshape(1, -1),
    )
    lik, grad, w_sum = pl.pallas_call(
        functools.partial(kernel, n_sta, n_src, chunk),
        out_shape=(
            jax.ShapeDtypeStruct((windows, cols), F32),
            jax.ShapeDtypeStruct((rows, cols, lanes), BF16),
            jax.ShapeDtypeStruct((w_rows, lanes), F32),
        ),
        in_specs=[hbm] * 9,
        out_specs=(hbm,) * 3,
        scratch_shapes=[pltpu.VMEM(a.shape, a.dtype) for a in operands[1:]]
        + [
            pltpu.VMEM((windows, cols), F32),
            pltpu.VMEM((rows, cols, lanes), BF16),
            pltpu.VMEM((2 * LAYERS, span_s, cols, lanes), BF16),
            pltpu.VMEM((2 * LAYERS, rows, span_r, lanes), BF16),
            pltpu.VMEM((LAYERS, rows, cols, 3 * lanes), BF16),
            pltpu.VMEM((rows, cols, 3 * lanes), BF16),
            pltpu.VMEM((LAYERS, HALVES, nodes // HALVES, lanes), F32),
            pltpu.VMEM((2, HALVES, half * J, (half + 2 * HW) * J), BF16),
            pltpu.VMEM((2, G * cols, G * span_r), BF16),
            pltpu.VMEM((2, LAYERS, 3 * lanes, lanes), BF16),
            pltpu.VMEM((jw, nodes), BF16),
            pltpu.VMEM((nodes, jw), BF16),
            pltpu.VMEM((n_sta, 8, lanes), F32),
            pltpu.VMEM((w_rows, lanes), F32),
            pltpu.VMEM((n_sta, chunk, lanes), F32),
            pltpu.VMEM((n_src, chunk, lanes), F32),
            pltpu.VMEM((w_rows, lanes), F32),
            dma((11,)),
            dma((HALVES + 2,)),
            dma((2 * LAYERS, 2 + 2 * HALVES)),
            dma((2 * LAYERS, 2 + 2 * HALVES)),
            dma((n_sta,)),
            dma((n_sta,)),
            dma((n_sta,)),
            dma((n_sta,)),
            dma((n_src,)),
            dma((n_src,)),
            dma((n_sta,)),
            dma((n_sta,)),
        ],
        compiler_params=pltpu.CompilerParams(
            collective_id=0, has_side_effects=True, vmem_limit_bytes=VMEM
        ),
    )(*operands)
    factor = float(1.0 / np.sqrt(np.float32(rows * n_sta * cols * n_src)))
    lik, grad, w_total, v_total = pl.pallas_call(
        functools.partial(finish, factor),
        out_shape=(
            jax.ShapeDtypeStruct(lik.shape, F32),
            jax.ShapeDtypeStruct(grad.shape, BF16),
            jax.ShapeDtypeStruct(layer_weights.shape, F32),
            jax.ShapeDtypeStruct((1, feature), F32),
        ),
        in_specs=[hbm] * 3,
        out_specs=(hbm, hbm, vmem, vmem),
        scratch_shapes=[pltpu.VMEM(w_sum.shape, F32), dma((3,))],
        compiler_params=pltpu.CompilerParams(vmem_limit_bytes=VMEM),
    )(lik, grad, w_sum)
    return (lik, grad, w_total, v_total.reshape(feature))


def solution(mesh):
    in_specs = (P("sta", "src", None), P(), P(), P(), P(), P(None, "sta"), P(None, "src"), P(), P())
    out_specs = (P(None, "src"), P("sta", "src", None), P(), P())
    body = functools.partial(shards, mesh.shape["sta"], mesh.shape["src"])
    return jax.shard_map(body, mesh=mesh, in_specs=in_specs, out_specs=out_specs, check_vma=False)
```

```python
import functools

import jax
import jax.numpy as jnp
import numpy as np
from jax import lax
from jax.experimental import pallas as pl
from jax.experimental.pallas import tpu as pltpu
from jax.sharding import PartitionSpec as P

LAYERS = 2
HW = 16
J = 16
G = 4
HALVES = 2
VMEM = 60 * 1024 * 1024
MESH = pl.DeviceIdType.MESH
F32, BF16 = jnp.float32, jnp.bfloat16


def iota(shape, dim):
    return lax.broadcasted_iota(jnp.int32, shape, dim)


def ones_where(cond):
    return jnp.where(cond, 1.0, 0.0).astype(BF16)


def over(value, size):
    return lax.shift_right_logical(value, jnp.full(value.shape, size.bit_length() - 1, jnp.int32))


def within(value, size):
    return value & (size - 1)


def dot(a, b):
    return lax.dot_general(a, b, (((1,), (0,)), ((), ())), preferred_element_type=F32)


def dot_nt(a, b):
    return lax.dot_general(a, b, (((1,), (1,)), ((), ())), preferred_element_type=F32)


def dot_tn(a, b):
    return lax.dot_general(a, b, (((0,), (0,)), ((), ())), preferred_element_type=F32)


def coefs(lists, count_row, base, span):
    total_rows = lists.shape[1]
    count = jnp.broadcast_to(count_row, (span, total_rows))
    place = iota((span, total_rows), 0) + base
    total = jnp.zeros((span, total_rows), F32)
    for k in range(lists.shape[0]):
        hit = (place == lists[k : k + 1]) & (count > float(k))
        total = total + jnp.where(hit, 1.0, 0.0)
    return (total * (1.0 / count_row)).astype(BF16)


def kernel(
    n_sta,
    n_src,
    chunk,
    feat,
    slist_hbm,
    scnt_hbm,
    rlist_hbm,
    rcnt_hbm,
    picks_hbm,
    targets_hbm,
    weights_hbm,
    readout_hbm,
    lik_hbm,
    grad_hbm,
    w_hbm,
    slist,
    scnt,
    rlist,
    rcnt,
    picks,
    targets,
    weights,
    readout,
    lik_out,
    grad_out,
    hs,
    hr,
    x,
    xb,
    slope,
    ks,
    bd,
    wf,
    q,
    qt,
    lik_slots,
    w_local,
    sta_slots,
    src_slots,
    total,
    load_sem,
    out_sem,
    halo_send,
    halo_recv,
    lik_send,
    lik_recv,
    a_send,
    a_recv,
    b_send,
    b_recv,
    c_send,
    c_recv,
):
    me_sta = lax.axis_index("sta")
    me_src = lax.axis_index("src")
    rows, cols, lanes = feat.shape
    feature = weights.shape[-1]
    windows = lanes // feature
    half = rows // HALVES
    span_s, span_r, span_h = rows + 2 * HW, cols + 2 * HW, half + 2 * HW
    nodes, part_nodes = rows * cols, half * cols
    all_sta, all_src = rows * n_sta, cols * n_src
    sta_first, src_first = me_sta * rows, me_src * cols

    def sta_peer(d):
        return lax.rem(me_sta + d, n_sta)

    def src_peer(d):
        return lax.rem(me_src + d, n_src)

    loads = [
        pltpu.make_async_copy(feat, hs.at[0, HW : HW + rows], load_sem.at[0]),
    ]
    pairs = [
        (slist_hbm, slist),
        (scnt_hbm, scnt),
        (rlist_hbm, rlist),
        (rcnt_hbm, rcnt),
        (picks_hbm, picks),
        (targets_hbm, targets),
        (weights_hbm, weights),
        (readout_hbm, readout),
    ]
    small = [pltpu.make_async_copy(a, b, load_sem.at[1 + n]) for n, (a, b) in enumerate(pairs)]
    for copy in small + loads:
        copy.start()

    for e in range(2 * LAYERS):
        zero_s = jnp.zeros((HW, cols, lanes), BF16)
        zero_r = jnp.zeros((rows, HW, lanes), BF16)

        @pl.when(me_sta == 0)
        def _():
            hs[e, 0:HW] = zero_s

        @pl.when(me_sta == n_sta - 1)
        def _():
            hs[e, HW + rows :] = zero_s

        @pl.when(me_src == 0)
        def _():
            hr[e, :, 0:HW] = zero_r

        @pl.when(me_src == n_src - 1)
        def _():
            hr[e, :, HW + cols :] = zero_r

    barrier = pltpu.get_barrier_semaphore()
    for d in range(1, n_sta):
        pl.semaphore_signal(barrier, inc=1, device_id={"sta": sta_peer(d)}, device_id_type=MESH)
    for d in range(1, n_src):
        pl.semaphore_signal(barrier, inc=1, device_id={"src": src_peer(d)}, device_id_type=MESH)

    for copy in small:
        copy.wait()
    s_row, r_row = scnt[...].astype(F32), rcnt[...].astype(F32)
    s_lists, r_lists = slist[...], rlist[...]
    same_col = within(iota((half * J, span_h * J), 0), J) == within(iota((half * J, span_h * J), 1), J)
    same_grp = over(iota((G * cols, G * span_r), 0), cols) == over(iota((G * cols, G * span_r), 1), span_r)

    def put_mixes(way, left_s, cols_s, left_r, cols_r):
        left_s, left_r = left_s.astype(BF16), left_r.astype(BF16)
        for h in range(HALVES):
            right = cols_s[:, h * half * J : (h * half + span_h) * J]
            wide = dot(left_s[h * half * J : (h + 1) * half * J], right)
            ks[way, h] = jnp.where(same_col, wide, 0.0).astype(BF16)
        bd[way] = jnp.where(same_grp, dot(left_r, cols_r), 0.0).astype(BF16)

    def forward_mixes():
        fwd_s = coefs(s_lists, s_row, sta_first - HW, span_s)
        fwd_r = coefs(r_lists, r_row, src_first - HW, span_r)
        row_s = (rows * J, all_sta)
        row_r = (G * cols, all_src)
        put_mixes(
            0,
            dot_nt(ones_where(over(iota(row_s, 0), J) + sta_first == iota(row_s, 1)), fwd_s),
            ones_where(over(iota((span_s, span_s * J), 1), J) == iota((span_s, span_s * J), 0)),
            dot_nt(ones_where(within(iota(row_r, 0), cols) + src_first == iota(row_r, 1)), fwd_r),
            ones_where(within(iota((span_r, G * span_r), 1), span_r) == iota((span_r, G * span_r), 0)),
        )

    forward_mixes()
    pl.semaphore_wait(barrier, n_sta + n_src - 2)

    def halo_copy(e, direction):
        h = (direction - 2) // 2
        own = slice(h * half, (h + 1) * half)
        if direction == 0:
            dst, device = hs.at[e, HW + rows :], {"sta": me_sta - 1}
            src = hs.at[e, HW : 2 * HW]
        elif direction == 1:
            dst, device = hs.at[e, 0:HW], {"sta": me_sta + 1}
            src = hs.at[e, rows : HW + rows]
        elif direction % 2 == 0:
            dst, device = hr.at[e, own, HW + cols :], {"src": me_src - 1}
            src = hr.at[e, own, HW : 2 * HW]
        else:
            dst, device = hr.at[e, own, 0:HW], {"src": me_src + 1}
            src = hr.at[e, own, cols : HW + cols]
        return pltpu.make_async_remote_copy(
            src_ref=src,
            dst_ref=dst,
            send_sem=halo_send.at[e, direction],
            recv_sem=halo_recv.at[e, direction],
            device_id=device,
            device_id_type=MESH,
        )

    sides = [me_sta > 0, me_sta < n_sta - 1, me_src > 0, me_src < n_src - 1]

    def goes(direction):
        return sides[direction if direction < 2 else 2 + direction % 2]

    def comes(direction):
        return sides[1 - direction if direction < 2 else 3 - direction % 2]

    def halo_start(e, directions):
        for direction in directions:
            pl.when(goes(direction))(lambda: halo_copy(e, direction).start())

    def halo_wait(e, directions):
        for direction in directions:
            pl.when(comes(direction))(lambda: halo_copy(e, direction).wait_recv())

    def halo_drain(e):
        for direction in range(2 + 2 * HALVES):
            pl.when(goes(direction))(lambda: halo_copy(e, direction).wait_send())

    def halo_put(e, h, values):
        own = slice(h * half, (h + 1) * half)
        hr[e, own, HW : HW + cols] = values
        halo_start(e, (2 + 2 * h, 3 + 2 * h))
        hs[e, HW + h * half : HW + (h + 1) * half] = values
        halo_start(e, (h,))

    for copy in loads:
        copy.wait()
    states = hs[0, HW : HW + rows]
    hr[0, :, HW : HW + cols] = states
    for h in range(HALVES):
        halo_start(0, (2 + 2 * h, 3 + 2 * h))
    halo_start(0, (0, 1))
    x[0, :, :, 0:lanes] = states

    def backward_mixes():
        bwd_s = coefs(s_lists, s_row, sta_first, rows)
        bwd_r = coefs(r_lists, r_row, src_first, cols)
        col_s = (all_sta, span_s * J)
        col_r = (all_src, G * span_r)
        put_mixes(
            1,
            dot(ones_where(over(iota((rows * J, rows), 0), J) == iota((rows * J, rows), 1)), bwd_s),
            ones_where(over(iota(col_s, 1), J) + (sta_first - HW) == iota(col_s, 0)),
            dot(ones_where(within(iota((G * cols, cols), 0), cols) == iota((G * cols, cols), 1)), bwd_r),
            ones_where(within(iota(col_r, 1), span_r) + (src_first - HW) == iota(col_r, 0)),
        )

    spread = ones_where(within(iota((lanes, feature), 0), feature) == iota((lanes, feature), 1))
    first_window = iota((feature, lanes), 1) < feature

    def put_weights():
        count = LAYERS * 3
        stack = weights[...].reshape(count * feature, feature)
        wide = dot_nt(stack, spread)
        double = jnp.concatenate([weights[n // 3, n % 3] for n in range(count) for _ in range(2)], axis=0)
        eye = ones_where(iota((feature, feature), 0) == iota((feature, feature), 1))
        turned = dot_nt(eye, double)
        for n in range(count):
            l, p = n // 3, n % 3
            for way, m in (
                (0, wide[n * feature : (n + 1) * feature]),
                (1, turned[:, n * lanes : (n + 1) * lanes]),
            ):
                top = slice(p * lanes, p * lanes + feature)
                low = slice(p * lanes + feature, (p + 1) * lanes)
                wf[way, l, top] = jnp.where(first_window, m, 0.0).astype(BF16)
                wf[way, l, low] = jnp.where(first_window, 0.0, m).astype(BF16)

    put_weights()

    def mix_sta(way, e, h, out):
        own = slice(h * half, (h + 1) * half)
        for j in range(0, cols, J):
            part = hs[e, h * half : h * half + span_h, j : j + J, :].reshape(span_h * J, lanes)
            mixed = dot(ks[way, h], part).astype(BF16)
            out[own, j : j + J, lanes : 2 * lanes] = mixed.reshape(half, J, lanes)

    def mix_src(way, e, h, out):
        for g in range(h * half, (h + 1) * half, G):
            part = hr[e, g : g + G].reshape(G * span_r, lanes)
            mixed = dot(bd[way], part).astype(BF16)
            out[g : g + G, :, 2 * lanes :] = mixed.reshape(G, cols, lanes)

    wide_readout = dot_nt(readout[...], spread)
    jw = windows * cols
    node_own = iota((jw, lanes), 0)
    win_mask = over(node_own, cols) == over(iota((jw, lanes), 1), feature)
    diag = within(node_own, cols) == iota((jw, lanes), 1)

    def to_column(row_of):
        wide = jnp.concatenate(
            [jnp.broadcast_to(row_of(w), (cols, lanes)) for w in range(windows)], axis=0
        )
        return jnp.sum(jnp.where(diag, wide, 0.0), axis=1, keepdims=True)

    picked = picks[...].astype(F32)
    for l in range(LAYERS):
        if l == 1:
            backward_mixes()
            wide_picks = jnp.concatenate(
                [jnp.broadcast_to(picked[w : w + 1], (cols, rows)) for w in range(windows)], axis=0
            ).astype(BF16)
            sel = ones_where(over(iota((nodes, rows), 0), cols) == iota((nodes, rows), 1))
            at_q = within(iota((jw, nodes), 0), cols) == within(iota((jw, nodes), 1), cols)
            q[...] = jnp.where(at_q, dot_nt(wide_picks, sel), 0.0).astype(BF16)
            at_t = within(iota((nodes, jw), 0), cols) == within(iota((nodes, jw), 1), cols)
            qt[...] = jnp.where(at_t, dot_nt(sel, wide_picks), 0.0).astype(BF16)
        for h in range(HALVES):
            own = slice(h * half, (h + 1) * half)
            halo_wait(l, (1 - h,))
            mix_sta(0, l, h, x.at[l])
            z = dot(x[l, own, :, 0 : 2 * lanes].reshape(part_nodes, 2 * lanes), wf[0, l, 0 : 2 * lanes])
            halo_wait(l, (2 + 2 * h, 3 + 2 * h))
            mix_src(0, l, h, x.at[l])
            z = z + dot(x[l, own, :, 2 * lanes :].reshape(part_nodes, lanes), wf[0, l, 2 * lanes :])
            squashed = jnp.tanh(z)
            slope[l, h] = 1.0 - squashed * squashed
            before = x[l, own, :, 0:lanes].astype(F32)
            states = (before + squashed.reshape(half, cols, lanes)).astype(BF16)
            if l + 1 < LAYERS:
                halo_put(l + 1, h, states)
                x[l + 1, own, :, 0:lanes] = states
            else:
                xb[own, :, 0:lanes] = states

    heap = dot(q[...], xb[:, :, 0:lanes].reshape(nodes, lanes))
    score = jnp.sum(jnp.where(win_mask, heap * wide_readout, 0.0), axis=1, keepdims=True)
    flat = jnp.where(diag, score, 0.0)
    tile_row = iota((8, lanes), 0)
    tile = jnp.zeros((8, lanes), F32)
    for w in range(windows):
        part = jnp.sum(flat[w * cols : (w + 1) * cols], axis=0, keepdims=True)
        tile = jnp.where(tile_row == w, part, tile)
        count = jnp.sum(picked[w : w + 1], axis=1, keepdims=True)
        tile = jnp.where(tile_row == windows + w, count, tile)
    lik_slots[me_sta] = tile
    sends = []
    for d in range(1, n_sta):
        sends.append(
            pltpu.make_async_remote_copy(
                src_ref=lik_slots.at[me_sta],
                dst_ref=lik_slots.at[me_sta],
                send_sem=lik_send.at[d],
                recv_sem=lik_recv.at[d],
                device_id={"sta": sta_peer(d)},
                device_id_type=MESH,
            )
        )
        sends[-1].start()
    for copy in sends:
        copy.wait_recv()
    summed = lik_slots[0]
    for s in range(1, n_sta):
        summed = summed + lik_slots[s]
    root = jnp.sqrt(jnp.maximum(summed[windows : 2 * windows], 1.0))
    lik = summed[0:windows] / root
    lik_out[...] = lik[:, :cols]
    outs = [pltpu.make_async_copy(lik_out, lik_hbm, out_sem.at[HALVES])]
    outs[0].start()
    sig = jax.nn.sigmoid(lik)
    sig_col = to_column(lambda w: sig[w : w + 1])
    want = jnp.concatenate(
        [jnp.broadcast_to(targets[w : w + 1, :], (cols, cols)) for w in range(windows)], axis=0
    )
    diag_cols = within(iota((jw, cols), 0), cols) == iota((jw, cols), 1)
    want_col = jnp.sum(jnp.where(diag_cols, want, 0.0), axis=1, keepdims=True)
    err = (sig_col - want_col).astype(BF16).astype(F32)
    err_wide = jnp.where(win_mask, err, 0.0)
    v_row = jnp.sum(err_wide * heap, axis=0, keepdims=True)

    def put_delta(l, h, grad):
        delta = (grad * slope[l, h]).astype(BF16).reshape(half, cols, lanes)
        halo_put(2 * LAYERS - 1 - l, h, delta)
        xb[h * half : (h + 1) * half, :, 0:lanes] = delta

    grads = []
    for h in range(HALVES):
        spot = slice(h * part_nodes, (h + 1) * part_nodes)
        grads.append(dot(qt[spot], err_wide.astype(BF16)) * wide_readout)
        put_delta(LAYERS - 1, h, grads[h])

    def weight_sums(l):
        w_t = dot_tn(xb[:, :, 0:lanes].reshape(nodes, lanes), x[l].reshape(nodes, 3 * lanes))
        folded = []
        for p in range(3):
            both = jnp.where(
                first_window,
                w_t[0:feature, p * lanes : (p + 1) * lanes],
                w_t[feature:, p * lanes : (p + 1) * lanes],
            )
            folded.append(both + pltpu.roll(both, feature, 1))
        base = l * feature
        w_local[base : base + feature] = jnp.where(first_window, folded[0], folded[1])
        return folded[2]

    def chunk_of(ref, s):
        return ref.at[pl.ds(pl.multiple_of(s * chunk, 16), chunk)]

    first, second, third = [], [], []
    for l in reversed(range(LAYERS)):
        e = 2 * LAYERS - 1 - l
        if l == 1:
            kept = weight_sums(l)
        else:
            w_local[2 * feature : 3 * feature] = jnp.where(first_window, weight_sums(l), kept)
            w_local[3 * feature :] = jnp.broadcast_to(v_row, (w_local.shape[0] - 3 * feature, lanes))
            for d in range(1, n_sta):
                first.append(
                    pltpu.make_async_remote_copy(
                        src_ref=chunk_of(w_local, sta_peer(d)),
                        dst_ref=sta_slots.at[me_sta],
                        send_sem=a_send.at[d],
                        recv_sem=a_recv.at[d],
                        device_id={"sta": sta_peer(d)},
                        device_id_type=MESH,
                    )
                )
                first[-1].start()
            sta_slots[me_sta] = chunk_of(w_local, me_sta)[...]
        for h in range(HALVES):
            own = slice(h * half, (h + 1) * half)
            halo_wait(e, (1 - h,))
            mix_sta(1, e, h, xb)
            if l == 0 and h == 0:
                for copy in first:
                    copy.wait_recv()
                some = sta_slots[0]
                for s in range(1, n_sta):
                    some = some + sta_slots[s]
                src_slots[me_src] = some.astype(BF16)
                for d in range(1, n_src):
                    second.append(
                        pltpu.make_async_remote_copy(
                            src_ref=src_slots.at[me_src],
                            dst_ref=src_slots.at[me_src],
                            send_sem=b_send.at[d],
                            recv_sem=b_recv.at[d],
                            device_id={"src": src_peer(d)},
                            device_id_type=MESH,
                        )
                    )
                    second[-1].start()
            early = xb[own, :, 0 : 2 * lanes].reshape(part_nodes, 2 * lanes)
            grad = grads[h] + dot(early, wf[1, l, 0 : 2 * lanes])
            halo_wait(e, (2 + 2 * h, 3 + 2 * h))
            mix_src(1, e, h, xb)
            late = xb[own, :, 2 * lanes :].reshape(part_nodes, lanes)
            grad = grad + dot(late, wf[1, l, 2 * lanes :])
            if l > 0:
                grads[h] = grad
                put_delta(l - 1, h, grad)
            else:
                grad_out[own] = grad.reshape(half, cols, lanes).astype(BF16)
                outs.append(pltpu.make_async_copy(grad_out.at[own], grad_hbm.at[own], out_sem.at[h]))
                outs[-1].start()

    for copy in second:
        copy.wait_recv()
    some = src_slots[0].astype(F32)
    for s in range(1, n_src):
        some = some + src_slots[s].astype(F32)
    chunk_of(total, me_sta)[...] = some
    for d in range(1, n_sta):
        third.append(
            pltpu.make_async_remote_copy(
                src_ref=chunk_of(total, me_sta),
                dst_ref=chunk_of(total, me_sta),
                send_sem=c_send.at[d],
                recv_sem=c_recv.at[d],
                device_id={"sta": sta_peer(d)},
                device_id_type=MESH,
            )
        )
        third[-1].start()
    for e in range(2 * LAYERS):
        halo_drain(e)
    for copy in sends + first + second:
        copy.wait_send()
    for copy in third:
        copy.wait_recv()
    outs.append(pltpu.make_async_copy(total, w_hbm, out_sem.at[HALVES + 1]))
    outs[-1].start()
    for copy in third:
        copy.wait_send()
    for copy in outs:
        copy.wait()


def finish(factor, lik, grad, w_sum, lik_out, grad_out, w_out, v_out, lik_buf, grad_buf, sums, sems):
    loads = [
        pltpu.make_async_copy(src, dst, sems.at[0, n])
        for n, (src, dst) in enumerate(((grad, grad_buf), (w_sum, sums), (lik, lik_buf)))
    ]
    stores = [
        pltpu.make_async_copy(src, dst, sems.at[1, n])
        for n, (src, dst) in enumerate(((grad_buf, grad_out), (lik_buf, lik_out)))
    ]
    for copy in loads:
        copy.start()
    loads[0].wait()
    stores[0].start()
    loads[2].wait()
    stores[1].start()
    loads[1].wait()
    feature = w_out.shape[-1]
    for t in range(3):
        turned = jnp.transpose(sums[t * feature : (t + 1) * feature] * factor)
        for n in range(2):
            l, p = (t, n) if t < 2 else (n, 2)
            w_out[l, p] = turned[n * feature : (n + 1) * feature]
    row = sums[3 * feature : 3 * feature + 1] * factor
    v_out[...] = (row + pltpu.roll(row, feature, 1))[:, :feature]
    for copy in stores:
        copy.wait()


def shards(
    n_sta,
    n_src,
    features,
    station_lists,
    station_counts,
    source_lists,
    source_counts,
    picks,
    targets,
    layer_weights,
    readout_vector,
):
    rows, cols, lanes = features.shape
    feature = layer_weights.shape[-1]
    windows = lanes // feature
    nodes = rows * cols
    half = rows // HALVES
    span_s, span_r = rows + 2 * HW, cols + 2 * HW
    chunk = -(-(3 * feature + 1) // (16 * n_sta)) * 16
    w_rows = chunk * n_sta
    jw = windows * cols
    dma = pltpu.SemaphoreType.DMA
    hbm = pl.BlockSpec(memory_space=pl.ANY)
    vmem = pl.BlockSpec(memory_space=pltpu.VMEM)
    operands = (
        features,
        station_lists.T,
        station_counts.reshape(1, -1),
        source_lists.T,
        source_counts.reshape(1, -1),
        picks,
        targets,
        layer_weights,
        readout_vector.reshape(1, -1),
    )
    lik, grad, w_sum = pl.pallas_call(
        functools.partial(kernel, n_sta, n_src, chunk),
        out_shape=(
            jax.ShapeDtypeStruct((windows, cols), F32),
            jax.ShapeDtypeStruct((rows, cols, lanes), BF16),
            jax.ShapeDtypeStruct((w_rows, lanes), F32),
        ),
        in_specs=[hbm] * 9,
        out_specs=(hbm,) * 3,
        scratch_shapes=[pltpu.VMEM(a.shape, a.dtype) for a in operands[1:]]
        + [
            pltpu.VMEM((windows, cols), F32),
            pltpu.VMEM((rows, cols, lanes), BF16),
            pltpu.VMEM((2 * LAYERS, span_s, cols, lanes), BF16),
            pltpu.VMEM((2 * LAYERS, rows, span_r, lanes), BF16),
            pltpu.VMEM((LAYERS, rows, cols, 3 * lanes), BF16),
            pltpu.VMEM((rows, cols, 3 * lanes), BF16),
            pltpu.VMEM((LAYERS, HALVES, nodes // HALVES, lanes), F32),
            pltpu.VMEM((2, HALVES, half * J, (half + 2 * HW) * J), BF16),
            pltpu.VMEM((2, G * cols, G * span_r), BF16),
            pltpu.VMEM((2, LAYERS, 3 * lanes, lanes), BF16),
            pltpu.VMEM((jw, nodes), BF16),
            pltpu.VMEM((nodes, jw), BF16),
            pltpu.VMEM((n_sta, 8, lanes), F32),
            pltpu.VMEM((w_rows, lanes), F32),
            pltpu.VMEM((n_sta, chunk, lanes), F32),
            pltpu.VMEM((n_src, chunk, lanes), BF16),
            pltpu.VMEM((w_rows, lanes), F32),
            dma((9,)),
            dma((HALVES + 2,)),
            dma((2 * LAYERS, 2 + 2 * HALVES)),
            dma((2 * LAYERS, 2 + 2 * HALVES)),
            dma((n_sta,)),
            dma((n_sta,)),
            dma((n_sta,)),
            dma((n_sta,)),
            dma((n_src,)),
            dma((n_src,)),
            dma((n_sta,)),
            dma((n_sta,)),
        ],
        compiler_params=pltpu.CompilerParams(
            collective_id=0, has_side_effects=True, vmem_limit_bytes=VMEM
        ),
    )(*operands)
    factor = float(1.0 / np.sqrt(np.float32(rows * n_sta * cols * n_src)))
    lik, grad, w_total, v_total = pl.pallas_call(
        functools.partial(finish, factor),
        out_shape=(
            jax.ShapeDtypeStruct(lik.shape, F32),
            jax.ShapeDtypeStruct(grad.shape, BF16),
            jax.ShapeDtypeStruct(layer_weights.shape, F32),
            jax.ShapeDtypeStruct((1, feature), F32),
        ),
        in_specs=[hbm] * 3,
        out_specs=(hbm, hbm, vmem, vmem),
        scratch_shapes=[
            pltpu.VMEM(lik.shape, F32),
            pltpu.VMEM(grad.shape, BF16),
            pltpu.VMEM(w_sum.shape, F32),
            dma((2, 3)),
        ],
        compiler_params=pltpu.CompilerParams(vmem_limit_bytes=VMEM),
    )(lik, grad, w_sum)
    return (lik, grad, w_total, v_total.reshape(feature))


def solution(mesh):
    in_specs = (P("sta", "src", None), P(), P(), P(), P(), P(None, "sta"), P(None, "src"), P(), P())
    out_specs = (P(None, "src"), P("sta", "src", None), P(), P())
    body = functools.partial(shards, mesh.shape["sta"], mesh.shape["src"])
    return jax.shard_map(body, mesh=mesh, in_specs=in_specs, out_specs=out_specs, check_vma=False)
```

```python
import functools

import jax
import jax.numpy as jnp
import numpy as np
from jax import lax
from jax.experimental import pallas as pl
from jax.experimental.pallas import tpu as pltpu
from jax.sharding import PartitionSpec as P

LAYERS = 2
HW = 16
J = 16
G = 4
HALVES = 2
VMEM = 60 * 1024 * 1024
MESH = pl.DeviceIdType.MESH
F32, BF16 = jnp.float32, jnp.bfloat16


def iota(shape, dim):
    return lax.broadcasted_iota(jnp.int32, shape, dim)


def ones_where(cond):
    return jnp.where(cond, 1.0, 0.0).astype(BF16)


def over(value, size):
    return lax.shift_right_logical(value, jnp.full(value.shape, size.bit_length() - 1, jnp.int32))


def within(value, size):
    return value & (size - 1)


def dot(a, b):
    return lax.dot_general(a, b, (((1,), (0,)), ((), ())), preferred_element_type=F32)


def dot_nt(a, b):
    return lax.dot_general(a, b, (((1,), (1,)), ((), ())), preferred_element_type=F32)


def dot_tn(a, b):
    return lax.dot_general(a, b, (((0,), (0,)), ((), ())), preferred_element_type=F32)


def coefs(lists, count_row, base, span):
    total_rows = lists.shape[1]
    count = jnp.broadcast_to(count_row, (span, total_rows))
    place = iota((span, total_rows), 0) + base
    total = jnp.zeros((span, total_rows), F32)
    for k in range(lists.shape[0]):
        hit = (place == lists[k : k + 1]) & (count > float(k))
        total = total + jnp.where(hit, 1.0, 0.0)
    return (total * (1.0 / count_row)).astype(BF16)


def kernel(
    n_sta,
    n_src,
    chunk,
    feat,
    slist_hbm,
    scnt_hbm,
    rlist_hbm,
    rcnt_hbm,
    picks_hbm,
    targets_hbm,
    weights_hbm,
    readout_hbm,
    lik_hbm,
    grad_hbm,
    w_hbm,
    slist,
    scnt,
    rlist,
    rcnt,
    picks,
    targets,
    weights,
    readout,
    lik_out,
    grad_out,
    hs,
    hr,
    x,
    xb,
    slope,
    ks,
    bd,
    wf,
    q,
    lik_slots,
    w_local,
    sta_slots,
    src_slots,
    total,
    load_sem,
    out_sem,
    halo_send,
    halo_recv,
    lik_send,
    lik_recv,
    a_send,
    a_recv,
    b_send,
    b_recv,
    c_send,
    c_recv,
):
    me_sta = lax.axis_index("sta")
    me_src = lax.axis_index("src")
    rows, cols, lanes = feat.shape
    feature = weights.shape[-1]
    windows = lanes // feature
    half = rows // HALVES
    span_s, span_r, span_h = rows + 2 * HW, cols + 2 * HW, half + 2 * HW
    nodes, part_nodes = rows * cols, half * cols
    all_sta, all_src = rows * n_sta, cols * n_src
    sta_first, src_first = me_sta * rows, me_src * cols

    def sta_peer(d):
        return lax.rem(me_sta + d, n_sta)

    def src_peer(d):
        return lax.rem(me_src + d, n_src)

    loads = [
        pltpu.make_async_copy(feat, hs.at[0, HW : HW + rows], load_sem.at[0]),
    ]
    pairs = [
        (slist_hbm, slist),
        (scnt_hbm, scnt),
        (rlist_hbm, rlist),
        (rcnt_hbm, rcnt),
        (picks_hbm, picks),
        (targets_hbm, targets),
        (weights_hbm, weights),
        (readout_hbm, readout),
    ]
    small = [pltpu.make_async_copy(a, b, load_sem.at[1 + n]) for n, (a, b) in enumerate(pairs)]
    for copy in small + loads:
        copy.start()

    for e in range(2 * LAYERS):
        zero_s = jnp.zeros((HW, cols, lanes), BF16)
        zero_r = jnp.zeros((rows, HW, lanes), BF16)

        @pl.when(me_sta == 0)
        def _():
            hs[e, 0:HW] = zero_s

        @pl.when(me_sta == n_sta - 1)
        def _():
            hs[e, HW + rows :] = zero_s

        @pl.when(me_src == 0)
        def _():
            hr[e, :, 0:HW] = zero_r

        @pl.when(me_src == n_src - 1)
        def _():
            hr[e, :, HW + cols :] = zero_r

    no_tiles = jnp.zeros((n_sta, 8, lanes), F32)

    @pl.when(me_src == 0)
    def _():
        lik_slots[1] = no_tiles

    @pl.when(me_src == n_src - 1)
    def _():
        lik_slots[2] = no_tiles

    barrier = pltpu.get_barrier_semaphore()
    for d in range(1, n_sta):
        pl.semaphore_signal(barrier, inc=1, device_id={"sta": sta_peer(d)}, device_id_type=MESH)
    for d in range(1, n_src):
        pl.semaphore_signal(barrier, inc=1, device_id={"src": src_peer(d)}, device_id_type=MESH)

    beside = ((me_src > 0, -1), (me_src < n_src - 1, 1))
    for near, step in beside:

        @pl.when(near)
        def _():
            for d in range(1, n_sta):
                pl.semaphore_signal(
                    barrier,
                    inc=1,
                    device_id={"sta": sta_peer(d), "src": me_src + step},
                    device_id_type=MESH,
                )

    for copy in small:
        copy.wait()
    s_row, r_row = scnt[...].astype(F32), rcnt[...].astype(F32)
    s_lists, r_lists = slist[...], rlist[...]
    same_col = within(iota((half * J, span_h * J), 0), J) == within(iota((half * J, span_h * J), 1), J)
    same_grp = over(iota((G * cols, G * span_r), 0), cols) == over(iota((G * cols, G * span_r), 1), span_r)

    def put_mixes(way, left_s, cols_s, left_r, cols_r):
        left_s, left_r = left_s.astype(BF16), left_r.astype(BF16)
        for h in range(HALVES):
            right = cols_s[:, h * half * J : (h * half + span_h) * J]
            wide = dot(left_s[h * half * J : (h + 1) * half * J], right)
            ks[way, h] = jnp.where(same_col, wide, 0.0).astype(BF16)
        bd[way] = jnp.where(same_grp, dot(left_r, cols_r), 0.0).astype(BF16)

    def forward_mixes():
        fwd_s = coefs(s_lists, s_row, sta_first - HW, span_s)
        fwd_r = coefs(r_lists, r_row, src_first - HW, span_r)
        row_s = (rows * J, all_sta)
        row_r = (G * cols, all_src)
        put_mixes(
            0,
            dot_nt(ones_where(over(iota(row_s, 0), J) + sta_first == iota(row_s, 1)), fwd_s),
            ones_where(over(iota((span_s, span_s * J), 1), J) == iota((span_s, span_s * J), 0)),
            dot_nt(ones_where(within(iota(row_r, 0), cols) + src_first == iota(row_r, 1)), fwd_r),
            ones_where(within(iota((span_r, G * span_r), 1), span_r) == iota((span_r, G * span_r), 0)),
        )

    forward_mixes()
    blocks_beside = (me_src > 0).astype(jnp.int32) + (me_src < n_src - 1).astype(jnp.int32)
    pl.semaphore_wait(barrier, n_sta + n_src - 2 + (n_sta - 1) * blocks_beside)

    def halo_copy(e, direction):
        h = (direction - 2) // 2
        own = slice(h * half, (h + 1) * half)
        if direction == 0:
            dst, device = hs.at[e, HW + rows :], {"sta": me_sta - 1}
            src = hs.at[e, HW : 2 * HW]
        elif direction == 1:
            dst, device = hs.at[e, 0:HW], {"sta": me_sta + 1}
            src = hs.at[e, rows : HW + rows]
        elif direction % 2 == 0:
            dst, device = hr.at[e, own, HW + cols :], {"src": me_src - 1}
            src = hr.at[e, own, HW : 2 * HW]
        else:
            dst, device = hr.at[e, own, 0:HW], {"src": me_src + 1}
            src = hr.at[e, own, cols : HW + cols]
        return pltpu.make_async_remote_copy(
            src_ref=src,
            dst_ref=dst,
            send_sem=halo_send.at[e, direction],
            recv_sem=halo_recv.at[e, direction],
            device_id=device,
            device_id_type=MESH,
        )

    sides = [me_sta > 0, me_sta < n_sta - 1, me_src > 0, me_src < n_src - 1]

    def goes(direction):
        return sides[direction if direction < 2 else 2 + direction % 2]

    def comes(direction):
        return sides[1 - direction if direction < 2 else 3 - direction % 2]

    def halo_start(e, directions):
        for direction in directions:
            pl.when(goes(direction))(lambda: halo_copy(e, direction).start())

    def halo_wait(e, directions):
        for direction in directions:
            pl.when(comes(direction))(lambda: halo_copy(e, direction).wait_recv())

    def halo_drain(e):
        for direction in range(2 + 2 * HALVES):
            pl.when(goes(direction))(lambda: halo_copy(e, direction).wait_send())

    def halo_put(e, h, values):
        own = slice(h * half, (h + 1) * half)
        hr[e, own, HW : HW + cols] = values
        halo_start(e, (2 + 2 * h, 3 + 2 * h))
        hs[e, HW + h * half : HW + (h + 1) * half] = values
        halo_start(e, (h,))

    for copy in loads:
        copy.wait()
    states = hs[0, HW : HW + rows]
    hr[0, :, HW : HW + cols] = states
    for h in range(HALVES):
        halo_start(0, (2 + 2 * h, 3 + 2 * h))
    halo_start(0, (0, 1))
    x[0, :, :, 0:lanes] = states

    def backward_mixes():
        bwd_s = coefs(s_lists, s_row, sta_first, rows)
        bwd_r = coefs(r_lists, r_row, src_first, cols)
        col_s = (all_sta, span_s * J)
        col_r = (all_src, G * span_r)
        put_mixes(
            1,
            dot(ones_where(over(iota((rows * J, rows), 0), J) == iota((rows * J, rows), 1)), bwd_s),
            ones_where(over(iota(col_s, 1), J) + (sta_first - HW) == iota(col_s, 0)),
            dot(ones_where(within(iota((G * cols, cols), 0), cols) == iota((G * cols, cols), 1)), bwd_r),
            ones_where(within(iota(col_r, 1), span_r) + (src_first - HW) == iota(col_r, 0)),
        )

    spread = ones_where(within(iota((lanes, feature), 0), feature) == iota((lanes, feature), 1))
    first_window = iota((feature, lanes), 1) < feature

    def put_weights():
        count = LAYERS * 3
        stack = weights[...].reshape(count * feature, feature)
        wide = dot_nt(stack, spread)
        double = jnp.concatenate([weights[n // 3, n % 3] for n in range(count) for _ in range(2)], axis=0)
        eye = ones_where(iota((feature, feature), 0) == iota((feature, feature), 1))
        turned = dot_nt(eye, double)
        for n in range(count):
            l, p = n // 3, n % 3
            for way, m in (
                (0, wide[n * feature : (n + 1) * feature]),
                (1, turned[:, n * lanes : (n + 1) * lanes]),
            ):
                top = slice(p * lanes, p * lanes + feature)
                low = slice(p * lanes + feature, (p + 1) * lanes)
                wf[way, l, top] = jnp.where(first_window, m, 0.0).astype(BF16)
                wf[way, l, low] = jnp.where(first_window, 0.0, m).astype(BF16)

    put_weights()

    def mix_sta(way, e, h, out):
        own = slice(h * half, (h + 1) * half)
        for j in range(0, cols, J):
            part = hs[e, h * half : h * half + span_h, j : j + J, :].reshape(span_h * J, lanes)
            mixed = dot(ks[way, h], part).astype(BF16)
            out[own, j : j + J, lanes : 2 * lanes] = mixed.reshape(half, J, lanes)

    def mix_src(way, e, h, out):
        for g in range(h * half, (h + 1) * half, G):
            part = hr[e, g : g + G].reshape(G * span_r, lanes)
            mixed = dot(bd[way], part).astype(BF16)
            out[g : g + G, :, 2 * lanes :] = mixed.reshape(G, cols, lanes)

    wide_readout = dot_nt(readout[...], spread)
    jw = windows * cols
    node_own = iota((jw, lanes), 0)
    win_mask = over(node_own, cols) == over(iota((jw, lanes), 1), feature)
    diag = within(node_own, cols) == iota((jw, lanes), 1)

    picked = picks[...].astype(F32)
    for l in range(LAYERS):
        if l == 1:
            backward_mixes()
            wide_picks = jnp.concatenate(
                [jnp.broadcast_to(picked[w : w + 1], (cols, rows)) for w in range(windows)], axis=0
            ).astype(BF16)
            sel = ones_where(over(iota((nodes, rows), 0), cols) == iota((nodes, rows), 1))
            at_q = within(iota((jw, nodes), 0), cols) == within(iota((jw, nodes), 1), cols)
            q[...] = jnp.where(at_q, dot_nt(wide_picks, sel), 0.0).astype(BF16)
        for h in range(HALVES):
            own = slice(h * half, (h + 1) * half)
            halo_wait(l, (1 - h,))
            mix_sta(0, l, h, x.at[l])
            z = dot(x[l, own, :, 0 : 2 * lanes].reshape(part_nodes, 2 * lanes), wf[0, l, 0 : 2 * lanes])
            halo_wait(l, (2 + 2 * h, 3 + 2 * h))
            mix_src(0, l, h, x.at[l])
            z = z + dot(x[l, own, :, 2 * lanes :].reshape(part_nodes, lanes), wf[0, l, 2 * lanes :])
            squashed = jnp.tanh(z)
            slopes = 1.0 - squashed * squashed
            slope[l, h] = slopes
            if l == LAYERS - 1:
                halo_put(LAYERS, h, slopes.astype(BF16).reshape(half, cols, lanes))
            before = x[l, own, :, 0:lanes].astype(F32)
            states = (before + squashed.reshape(half, cols, lanes)).astype(BF16)
            if l + 1 < LAYERS:
                halo_put(l + 1, h, states)
                x[l + 1, own, :, 0:lanes] = states
            else:
                xb[own, :, 0:lanes] = states

    heap = dot(q[...], xb[:, :, 0:lanes].reshape(nodes, lanes))
    score = jnp.sum(jnp.where(win_mask, heap * wide_readout, 0.0), axis=1, keepdims=True)
    flat = jnp.where(diag, score, 0.0)
    tile_row = iota((8, lanes), 0)
    tile = jnp.zeros((8, lanes), F32)
    for w in range(windows):
        part = jnp.sum(flat[w * cols : (w + 1) * cols], axis=0, keepdims=True)
        tile = jnp.where(tile_row == w, part, tile)
        count = jnp.sum(picked[w : w + 1], axis=1, keepdims=True)
        tile = jnp.where(tile_row == windows + w, count, tile)
    lik_slots[0, me_sta] = tile
    lik_slots[0, me_sta, 2 * windows : 3 * windows, 0:rows] = picked
    lik_slots[0, me_sta, 3 * windows : 4 * windows, 0:cols] = targets[...]

    def tile_copy(slot, d):
        return pltpu.make_async_remote_copy(
            src_ref=lik_slots.at[0, me_sta],
            dst_ref=lik_slots.at[slot, me_sta],
            send_sem=lik_send.at[slot, d],
            recv_sem=lik_recv.at[slot, d],
            device_id={"sta": sta_peer(d), "src": me_src + (0, 1, -1)[slot]},
            device_id_type=MESH,
        )

    def tiles(act, coming):
        for d in range(1, n_sta):
            act(tile_copy(0, d))
        for slot, side in ((1, 2 if coming else 3), (2, 3 if coming else 2)):

            @pl.when(sides[side])
            def _():
                for d in range(n_sta):
                    act(tile_copy(slot, d))

    tiles(lambda copy: copy.start(), False)
    halo_wait(LAYERS, range(2 + 2 * HALVES))
    halo_drain(LAYERS)
    tiles(lambda copy: copy.wait_recv(), True)

    lane_window = over(iota((8, lanes), 1), feature)

    def turn(values, row):
        return dot_tn(values, jnp.where(tile_row == row + lane_window, 1.0, 0.0))

    def error_of(slot):
        summed = lik_slots[slot, 0]
        for s in range(1, n_sta):
            summed = summed + lik_slots[slot, s]
        root = jnp.sqrt(jnp.maximum(summed[windows : 2 * windows], 1.0))
        lik = summed[0:windows] / root
        want = lik_slots[slot, 0, 3 * windows : 4 * windows]
        err = (jax.nn.sigmoid(lik) - want).astype(BF16).astype(F32)
        err = jnp.concatenate([err, jnp.zeros((8 - windows, lanes), F32)], axis=0)
        return lik, turn(err, 0)[:cols]

    lik, err_own = error_of(0)
    lik_out[...] = lik[:, :cols]
    outs = [pltpu.make_async_copy(lik_out, lik_hbm, out_sem.at[HALVES])]
    outs[0].start()
    heap_own = jnp.where(win_mask, heap, 0.0)
    heap_sum = heap_own[0:cols]
    for w in range(1, windows):
        heap_sum = heap_sum + heap_own[w * cols : (w + 1) * cols]
    v_row = jnp.sum(err_own * heap_sum, axis=0, keepdims=True)
    err_own = err_own * wide_readout
    err_left = error_of(1)[1][cols - HW :] * wide_readout
    err_right = error_of(2)[1][:HW] * wide_readout
    picks_own = turn(lik_slots[0, me_sta], 2 * windows)
    picks_up = turn(lik_slots[0, sta_peer(n_sta - 1)], 2 * windows)
    picks_down = turn(lik_slots[0, sta_peer(1)], 2 * windows)

    top = LAYERS

    def put_delta(l, h, grad):
        delta = (grad * slope[l, h]).astype(BF16).reshape(half, cols, lanes)
        if l == LAYERS - 1:
            hr[top, h * half : (h + 1) * half, HW : HW + cols] = delta
            hs[top, HW + h * half : HW + (h + 1) * half] = delta
        else:
            halo_put(2 * LAYERS - 1 - l, h, delta)
        xb[h * half : (h + 1) * half, :, 0:lanes] = delta

    def scaled(values, err, picked_row):
        return (values.astype(F32) * (err * picked_row)).astype(BF16)

    grads = []
    for h in range(HALVES):
        spots = range(h * half, (h + 1) * half)
        grads.append(jnp.concatenate([err_own * picks_own[i : i + 1] for i in spots], axis=0))
        put_delta(LAYERS - 1, h, grads[h])
    for m in range(HW):
        up = picks_up[rows - HW + m : rows - HW + m + 1]
        hs[top, m] = scaled(hs[top, m], err_own, up)
        hs[top, HW + rows + m] = scaled(hs[top, HW + rows + m], err_own, picks_down[m : m + 1])
    for i in range(rows):
        own_row = picks_own[i : i + 1]
        hr[top, i, 0:HW] = scaled(hr[top, i, 0:HW], err_left, own_row)
        hr[top, i, HW + cols :] = scaled(hr[top, i, HW + cols :], err_right, own_row)

    def weight_sums(l):
        w_t = dot_tn(xb[:, :, 0:lanes].reshape(nodes, lanes), x[l].reshape(nodes, 3 * lanes))
        folded = []
        for p in range(3):
            both = jnp.where(
                first_window,
                w_t[0:feature, p * lanes : (p + 1) * lanes],
                w_t[feature:, p * lanes : (p + 1) * lanes],
            )
            folded.append(both + pltpu.roll(both, feature, 1))
        base = l * feature
        w_local[base : base + feature] = jnp.where(first_window, folded[0], folded[1])
        return folded[2]

    def chunk_of(ref, s):
        return ref.at[pl.ds(pl.multiple_of(s * chunk, 16), chunk)]

    first, second, third = [], [], []
    for l in reversed(range(LAYERS)):
        e = 2 * LAYERS - 1 - l
        if l == 1:
            kept = weight_sums(l)
        else:
            w_local[2 * feature : 3 * feature] = jnp.where(first_window, weight_sums(l), kept)
            w_local[3 * feature :] = jnp.broadcast_to(v_row, (w_local.shape[0] - 3 * feature, lanes))
            for d in range(1, n_sta):
                first.append(
                    pltpu.make_async_remote_copy(
                        src_ref=chunk_of(w_local, sta_peer(d)),
                        dst_ref=sta_slots.at[me_sta],
                        send_sem=a_send.at[d],
                        recv_sem=a_recv.at[d],
                        device_id={"sta": sta_peer(d)},
                        device_id_type=MESH,
                    )
                )
                first[-1].start()
            sta_slots[me_sta] = chunk_of(w_local, me_sta)[...]
        for h in range(HALVES):
            own = slice(h * half, (h + 1) * half)
            if e > top:
                halo_wait(e, (1 - h,))
            mix_sta(1, e, h, xb)
            if l == 0 and h == 0:
                for copy in first:
                    copy.wait_recv()
                some = sta_slots[0]
                for s in range(1, n_sta):
                    some = some + sta_slots[s]
                src_slots[me_src] = some.astype(BF16)
                for d in range(1, n_src):
                    second.append(
                        pltpu.make_async_remote_copy(
                            src_ref=src_slots.at[me_src],
                            dst_ref=src_slots.at[me_src],
                            send_sem=b_send.at[d],
                            recv_sem=b_recv.at[d],
                            device_id={"src": src_peer(d)},
                            device_id_type=MESH,
                        )
                    )
                    second[-1].start()
            early = xb[own, :, 0 : 2 * lanes].reshape(part_nodes, 2 * lanes)
            grad = grads[h] + dot(early, wf[1, l, 0 : 2 * lanes])
            if e > top:
                halo_wait(e, (2 + 2 * h, 3 + 2 * h))
            mix_src(1, e, h, xb)
            late = xb[own, :, 2 * lanes :].reshape(part_nodes, lanes)
            grad = grad + dot(late, wf[1, l, 2 * lanes :])
            if l > 0:
                grads[h] = grad
                put_delta(l - 1, h, grad)
            else:
                grad_out[own] = grad.reshape(half, cols, lanes).astype(BF16)
                outs.append(pltpu.make_async_copy(grad_out.at[own], grad_hbm.at[own], out_sem.at[h]))
                outs[-1].start()

    for copy in second:
        copy.wait_recv()
    some = src_slots[0].astype(F32)
    for s in range(1, n_src):
        some = some + src_slots[s].astype(F32)
    chunk_of(total, me_sta)[...] = some
    for d in range(1, n_sta):
        third.append(
            pltpu.make_async_remote_copy(
                src_ref=chunk_of(total, me_sta),
                dst_ref=chunk_of(total, me_sta),
                send_sem=c_send.at[d],
                recv_sem=c_recv.at[d],
                device_id={"sta": sta_peer(d)},
                device_id_type=MESH,
            )
        )
        third[-1].start()
    for e in range(2 * LAYERS):
        if e != top:
            halo_drain(e)
    tiles(lambda copy: copy.wait_send(), False)
    for copy in first + second:
        copy.wait_send()
    for copy in third:
        copy.wait_recv()
    outs.append(pltpu.make_async_copy(total, w_hbm, out_sem.at[HALVES + 1]))
    outs[-1].start()
    for copy in third:
        copy.wait_send()
    for copy in outs:
        copy.wait()


def finish(factor, lik, grad, w_sum, lik_out, grad_out, w_out, v_out, lik_buf, grad_buf, sums, sems):
    loads = [
        pltpu.make_async_copy(src, dst, sems.at[0, n])
        for n, (src, dst) in enumerate(((grad, grad_buf), (w_sum, sums), (lik, lik_buf)))
    ]
    stores = [
        pltpu.make_async_copy(src, dst, sems.at[1, n])
        for n, (src, dst) in enumerate(((grad_buf, grad_out), (lik_buf, lik_out)))
    ]
    for copy in loads:
        copy.start()
    loads[0].wait()
    stores[0].start()
    loads[2].wait()
    stores[1].start()
    loads[1].wait()
    feature = w_out.shape[-1]
    for t in range(3):
        turned = jnp.transpose(sums[t * feature : (t + 1) * feature] * factor)
        for n in range(2):
            l, p = (t, n) if t < 2 else (n, 2)
            w_out[l, p] = turned[n * feature : (n + 1) * feature]
    row = sums[3 * feature : 3 * feature + 1] * factor
    v_out[...] = (row + pltpu.roll(row, feature, 1))[:, :feature]
    for copy in stores:
        copy.wait()


def shards(
    n_sta,
    n_src,
    features,
    station_lists,
    station_counts,
    source_lists,
    source_counts,
    picks,
    targets,
    layer_weights,
    readout_vector,
):
    rows, cols, lanes = features.shape
    feature = layer_weights.shape[-1]
    windows = lanes // feature
    nodes = rows * cols
    half = rows // HALVES
    span_s, span_r = rows + 2 * HW, cols + 2 * HW
    chunk = -(-(3 * feature + 1) // (16 * n_sta)) * 16
    w_rows = chunk * n_sta
    jw = windows * cols
    dma = pltpu.SemaphoreType.DMA
    hbm = pl.BlockSpec(memory_space=pl.ANY)
    vmem = pl.BlockSpec(memory_space=pltpu.VMEM)
    operands = (
        features,
        station_lists.T,
        station_counts.reshape(1, -1),
        source_lists.T,
        source_counts.reshape(1, -1),
        picks,
        targets,
        layer_weights,
        readout_vector.reshape(1, -1),
    )
    lik, grad, w_sum = pl.pallas_call(
        functools.partial(kernel, n_sta, n_src, chunk),
        out_shape=(
            jax.ShapeDtypeStruct((windows, cols), F32),
            jax.ShapeDtypeStruct((rows, cols, lanes), BF16),
            jax.ShapeDtypeStruct((w_rows, lanes), F32),
        ),
        in_specs=[hbm] * 9,
        out_specs=(hbm,) * 3,
        scratch_shapes=[pltpu.VMEM(a.shape, a.dtype) for a in operands[1:]]
        + [
            pltpu.VMEM((windows, cols), F32),
            pltpu.VMEM((rows, cols, lanes), BF16),
            pltpu.VMEM((2 * LAYERS, span_s, cols, lanes), BF16),
            pltpu.VMEM((2 * LAYERS, rows, span_r, lanes), BF16),
            pltpu.VMEM((LAYERS, rows, cols, 3 * lanes), BF16),
            pltpu.VMEM((rows, cols, 3 * lanes), BF16),
            pltpu.VMEM((LAYERS, HALVES, nodes // HALVES, lanes), F32),
            pltpu.VMEM((2, HALVES, half * J, (half + 2 * HW) * J), BF16),
            pltpu.VMEM((2, G * cols, G * span_r), BF16),
            pltpu.VMEM((2, LAYERS, 3 * lanes, lanes), BF16),
            pltpu.VMEM((jw, nodes), BF16),
            pltpu.VMEM((3, n_sta, 8, lanes), F32),
            pltpu.VMEM((w_rows, lanes), F32),
            pltpu.VMEM((n_sta, chunk, lanes), F32),
            pltpu.VMEM((n_src, chunk, lanes), BF16),
            pltpu.VMEM((w_rows, lanes), F32),
            dma((9,)),
            dma((HALVES + 2,)),
            dma((2 * LAYERS, 2 + 2 * HALVES)),
            dma((2 * LAYERS, 2 + 2 * HALVES)),
            dma((3, n_sta)),
            dma((3, n_sta)),
            dma((n_sta,)),
            dma((n_sta,)),
            dma((n_src,)),
            dma((n_src,)),
            dma((n_sta,)),
            dma((n_sta,)),
        ],
        compiler_params=pltpu.CompilerParams(
            collective_id=0, has_side_effects=True, vmem_limit_bytes=VMEM
        ),
    )(*operands)
    factor = float(1.0 / np.sqrt(np.float32(rows * n_sta * cols * n_src)))
    lik, grad, w_total, v_total = pl.pallas_call(
        functools.partial(finish, factor),
        out_shape=(
            jax.ShapeDtypeStruct(lik.shape, F32),
            jax.ShapeDtypeStruct(grad.shape, BF16),
            jax.ShapeDtypeStruct(layer_weights.shape, F32),
            jax.ShapeDtypeStruct((1, feature), F32),
        ),
        in_specs=[hbm] * 3,
        out_specs=(hbm, hbm, vmem, vmem),
        scratch_shapes=[
            pltpu.VMEM(lik.shape, F32),
            pltpu.VMEM(grad.shape, BF16),
            pltpu.VMEM(w_sum.shape, F32),
            dma((2, 3)),
        ],
        compiler_params=pltpu.CompilerParams(vmem_limit_bytes=VMEM),
    )(lik, grad, w_sum)
    return (lik, grad, w_total, v_total.reshape(feature))


def solution(mesh):
    in_specs = (P("sta", "src", None), P(), P(), P(), P(), P(None, "sta"), P(None, "src"), P(), P())
    out_specs = (P(None, "src"), P("sta", "src", None), P(), P())
    body = functools.partial(shards, mesh.shape["sta"], mesh.shape["src"])
    return jax.shard_map(body, mesh=mesh, in_specs=in_specs, out_specs=out_specs, check_vma=False)
```

```python
import functools

import jax
import jax.numpy as jnp
import numpy as np
from jax import lax
from jax.experimental import pallas as pl
from jax.experimental.pallas import tpu as pltpu
from jax.sharding import PartitionSpec as P

LAYERS = 2
HW = 16
J = 16
G = 4
HALVES = 2
VMEM = 60 * 1024 * 1024
MESH = pl.DeviceIdType.MESH
F32, BF16 = jnp.float32, jnp.bfloat16


def iota(shape, dim):
    return lax.broadcasted_iota(jnp.int32, shape, dim)


def ones_where(cond):
    return jnp.where(cond, 1.0, 0.0).astype(BF16)


def over(value, size):
    return lax.shift_right_logical(value, jnp.full(value.shape, size.bit_length() - 1, jnp.int32))


def within(value, size):
    return value & (size - 1)


def dot(a, b):
    return lax.dot_general(a, b, (((1,), (0,)), ((), ())), preferred_element_type=F32)


def dot_nt(a, b):
    return lax.dot_general(a, b, (((1,), (1,)), ((), ())), preferred_element_type=F32)


def dot_tn(a, b):
    return lax.dot_general(a, b, (((0,), (0,)), ((), ())), preferred_element_type=F32)


def coefs(lists, count_row, base, span):
    total_rows = lists.shape[1]
    count = jnp.broadcast_to(count_row, (span, total_rows))
    place = iota((span, total_rows), 0) + base
    total = jnp.zeros((span, total_rows), F32)
    for k in range(lists.shape[0]):
        hit = (place == lists[k : k + 1]) & (count > float(k))
        total = total + jnp.where(hit, 1.0, 0.0)
    return (total * (1.0 / count_row)).astype(BF16)


def kernel(
    n_sta,
    n_src,
    chunk,
    feat,
    slist_hbm,
    scnt_hbm,
    rlist_hbm,
    rcnt_hbm,
    picks_hbm,
    targets_hbm,
    weights_hbm,
    readout_hbm,
    lik_hbm,
    grad_hbm,
    w_hbm,
    slist,
    scnt,
    rlist,
    rcnt,
    picks,
    targets,
    weights,
    readout,
    lik_out,
    grad_out,
    hs,
    hr,
    x,
    xb,
    slope,
    ks,
    bd,
    wf,
    q,
    lik_slots,
    w_local,
    sta_slots,
    src_slots,
    total,
    load_sem,
    out_sem,
    halo_send,
    halo_recv,
    lik_send,
    lik_recv,
    a_send,
    a_recv,
    b_send,
    b_recv,
    c_send,
    c_recv,
):
    me_sta = lax.axis_index("sta")
    me_src = lax.axis_index("src")
    rows, cols, lanes = feat.shape
    feature = weights.shape[-1]
    windows = lanes // feature
    half = rows // HALVES
    span_s, span_r, span_h = rows + 2 * HW, cols + 2 * HW, half + 2 * HW
    nodes, part_nodes = rows * cols, half * cols
    all_sta, all_src = rows * n_sta, cols * n_src
    sta_first, src_first = me_sta * rows, me_src * cols

    def sta_peer(d):
        return lax.rem(me_sta + d, n_sta)

    def src_peer(d):
        return lax.rem(me_src + d, n_src)

    loads = [
        pltpu.make_async_copy(feat, hs.at[0, HW : HW + rows], load_sem.at[0]),
    ]
    pairs = [
        (slist_hbm, slist),
        (scnt_hbm, scnt),
        (rlist_hbm, rlist),
        (rcnt_hbm, rcnt),
        (picks_hbm, picks),
        (targets_hbm, targets),
        (weights_hbm, weights),
        (readout_hbm, readout),
    ]
    small = [pltpu.make_async_copy(a, b, load_sem.at[1 + n]) for n, (a, b) in enumerate(pairs)]
    for copy in small + loads:
        copy.start()

    for e in range(2 * LAYERS):
        zero_s = jnp.zeros((HW, cols, lanes), BF16)
        zero_r = jnp.zeros((rows, HW, lanes), BF16)

        @pl.when(me_sta == 0)
        def _():
            hs[e, 0:HW] = zero_s

        @pl.when(me_sta == n_sta - 1)
        def _():
            hs[e, HW + rows :] = zero_s

        @pl.when(me_src == 0)
        def _():
            hr[e, :, 0:HW] = zero_r

        @pl.when(me_src == n_src - 1)
        def _():
            hr[e, :, HW + cols :] = zero_r

    no_tiles = jnp.zeros((n_sta, 8, lanes), F32)

    @pl.when(me_src == 0)
    def _():
        lik_slots[1] = no_tiles

    @pl.when(me_src == n_src - 1)
    def _():
        lik_slots[2] = no_tiles

    barrier = pltpu.get_barrier_semaphore()
    for d in range(1, n_sta):
        pl.semaphore_signal(barrier, inc=1, device_id={"sta": sta_peer(d)}, device_id_type=MESH)
    for d in range(1, n_src):
        pl.semaphore_signal(barrier, inc=1, device_id={"src": src_peer(d)}, device_id_type=MESH)

    beside = ((me_src > 0, -1), (me_src < n_src - 1, 1))
    for near, step in beside:

        @pl.when(near)
        def _():
            for d in range(1, n_sta):
                pl.semaphore_signal(
                    barrier,
                    inc=1,
                    device_id={"sta": sta_peer(d), "src": me_src + step},
                    device_id_type=MESH,
                )

    for copy in small:
        copy.wait()
    s_row, r_row = scnt[...].astype(F32), rcnt[...].astype(F32)
    s_lists, r_lists = slist[...], rlist[...]
    same_col = within(iota((half * J, span_h * J), 0), J) == within(iota((half * J, span_h * J), 1), J)
    same_grp = over(iota((G * cols, G * span_r), 0), cols) == over(iota((G * cols, G * span_r), 1), span_r)

    def put_mixes(way, left_s, cols_s, left_r, cols_r):
        left_s, left_r = left_s.astype(BF16), left_r.astype(BF16)
        for h in range(HALVES):
            right = cols_s[:, h * half * J : (h * half + span_h) * J]
            wide = dot(left_s[h * half * J : (h + 1) * half * J], right)
            ks[way, h] = jnp.where(same_col, wide, 0.0).astype(BF16)
        bd[way] = jnp.where(same_grp, dot(left_r, cols_r), 0.0).astype(BF16)

    def forward_mixes():
        fwd_s = coefs(s_lists, s_row, sta_first - HW, span_s)
        fwd_r = coefs(r_lists, r_row, src_first - HW, span_r)
        row_s = (rows * J, all_sta)
        row_r = (G * cols, all_src)
        put_mixes(
            0,
            dot_nt(ones_where(over(iota(row_s, 0), J) + sta_first == iota(row_s, 1)), fwd_s),
            ones_where(over(iota((span_s, span_s * J), 1), J) == iota((span_s, span_s * J), 0)),
            dot_nt(ones_where(within(iota(row_r, 0), cols) + src_first == iota(row_r, 1)), fwd_r),
            ones_where(within(iota((span_r, G * span_r), 1), span_r) == iota((span_r, G * span_r), 0)),
        )

    forward_mixes()
    blocks_beside = (me_src > 0).astype(jnp.int32) + (me_src < n_src - 1).astype(jnp.int32)
    pl.semaphore_wait(barrier, n_sta + n_src - 2 + (n_sta - 1) * blocks_beside)

    def halo_copy(e, direction):
        h = (direction - 2) // 2
        own = slice(h * half, (h + 1) * half)
        if direction == 0:
            dst, device = hs.at[e, HW + rows :], {"sta": me_sta - 1}
            src = hs.at[e, HW : 2 * HW]
        elif direction == 1:
            dst, device = hs.at[e, 0:HW], {"sta": me_sta + 1}
            src = hs.at[e, rows : HW + rows]
        elif direction % 2 == 0:
            dst, device = hr.at[e, own, HW + cols :], {"src": me_src - 1}
            src = hr.at[e, own, HW : 2 * HW]
        else:
            dst, device = hr.at[e, own, 0:HW], {"src": me_src + 1}
            src = hr.at[e, own, cols : HW + cols]
        return pltpu.make_async_remote_copy(
            src_ref=src,
            dst_ref=dst,
            send_sem=halo_send.at[e, direction],
            recv_sem=halo_recv.at[e, direction],
            device_id=device,
            device_id_type=MESH,
        )

    sides = [me_sta > 0, me_sta < n_sta - 1, me_src > 0, me_src < n_src - 1]

    def goes(direction):
        return sides[direction if direction < 2 else 2 + direction % 2]

    def comes(direction):
        return sides[1 - direction if direction < 2 else 3 - direction % 2]

    def halo_start(e, directions):
        for direction in directions:
            pl.when(goes(direction))(lambda: halo_copy(e, direction).start())

    def halo_wait(e, directions):
        for direction in directions:
            pl.when(comes(direction))(lambda: halo_copy(e, direction).wait_recv())

    def halo_drain(e):
        for direction in range(2 + 2 * HALVES):
            pl.when(goes(direction))(lambda: halo_copy(e, direction).wait_send())

    def halo_put(e, h, values):
        own = slice(h * half, (h + 1) * half)
        hr[e, own, HW : HW + cols] = values
        halo_start(e, (2 + 2 * h, 3 + 2 * h))
        hs[e, HW + h * half : HW + (h + 1) * half] = values
        halo_start(e, (h,))

    for copy in loads:
        copy.wait()
    states = hs[0, HW : HW + rows]
    hr[0, :, HW : HW + cols] = states
    for h in range(HALVES):
        halo_start(0, (2 + 2 * h, 3 + 2 * h))
    halo_start(0, (0, 1))
    x[0, :, :, 0:lanes] = states

    def backward_mixes():
        bwd_s = coefs(s_lists, s_row, sta_first, rows)
        bwd_r = coefs(r_lists, r_row, src_first, cols)
        col_s = (all_sta, span_s * J)
        col_r = (all_src, G * span_r)
        put_mixes(
            1,
            dot(ones_where(over(iota((rows * J, rows), 0), J) == iota((rows * J, rows), 1)), bwd_s),
            ones_where(over(iota(col_s, 1), J) + (sta_first - HW) == iota(col_s, 0)),
            dot(ones_where(within(iota((G * cols, cols), 0), cols) == iota((G * cols, cols), 1)), bwd_r),
            ones_where(within(iota(col_r, 1), span_r) + (src_first - HW) == iota(col_r, 0)),
        )

    spread = ones_where(within(iota((lanes, feature), 0), feature) == iota((lanes, feature), 1))
    first_window = iota((feature, lanes), 1) < feature

    def put_weights():
        count = LAYERS * 3
        stack = weights[...].reshape(count * feature, feature)
        wide = dot_nt(stack, spread)
        double = jnp.concatenate([weights[n // 3, n % 3] for n in range(count) for _ in range(2)], axis=0)
        eye = ones_where(iota((feature, feature), 0) == iota((feature, feature), 1))
        turned = dot_nt(eye, double)
        for n in range(count):
            l, p = n // 3, n % 3
            for way, m in (
                (0, wide[n * feature : (n + 1) * feature]),
                (1, turned[:, n * lanes : (n + 1) * lanes]),
            ):
                top = slice(p * lanes, p * lanes + feature)
                low = slice(p * lanes + feature, (p + 1) * lanes)
                wf[way, l, top] = jnp.where(first_window, m, 0.0).astype(BF16)
                wf[way, l, low] = jnp.where(first_window, 0.0, m).astype(BF16)

    put_weights()

    def mix_sta(way, e, h, out):
        own = slice(h * half, (h + 1) * half)
        for j in range(0, cols, J):
            part = hs[e, h * half : h * half + span_h, j : j + J, :].reshape(span_h * J, lanes)
            mixed = dot(ks[way, h], part).astype(BF16)
            out[own, j : j + J, lanes : 2 * lanes] = mixed.reshape(half, J, lanes)

    def mix_src(way, e, h, out):
        for g in range(h * half, (h + 1) * half, G):
            part = hr[e, g : g + G].reshape(G * span_r, lanes)
            mixed = dot(bd[way], part).astype(BF16)
            out[g : g + G, :, 2 * lanes :] = mixed.reshape(G, cols, lanes)

    wide_readout = dot_nt(readout[...], spread)
    jw = windows * cols
    node_own = iota((jw, lanes), 0)
    win_mask = over(node_own, cols) == over(iota((jw, lanes), 1), feature)
    diag = within(node_own, cols) == iota((jw, lanes), 1)

    picked = picks[...].astype(F32)
    for l in range(LAYERS):
        if l == 1:
            backward_mixes()
            wide_picks = jnp.concatenate(
                [jnp.broadcast_to(picked[w : w + 1], (cols, rows)) for w in range(windows)], axis=0
            ).astype(BF16)
            sel = ones_where(over(iota((nodes, rows), 0), cols) == iota((nodes, rows), 1))
            at_q = within(iota((jw, nodes), 0), cols) == within(iota((jw, nodes), 1), cols)
            q[...] = jnp.where(at_q, dot_nt(wide_picks, sel), 0.0).astype(BF16)
        for h in range(HALVES):
            own = slice(h * half, (h + 1) * half)
            halo_wait(l, (1 - h,))
            mix_sta(0, l, h, x.at[l])
            z = dot(x[l, own, :, 0 : 2 * lanes].reshape(part_nodes, 2 * lanes), wf[0, l, 0 : 2 * lanes])
            halo_wait(l, (2 + 2 * h, 3 + 2 * h))
            mix_src(0, l, h, x.at[l])
            z = z + dot(x[l, own, :, 2 * lanes :].reshape(part_nodes, lanes), wf[0, l, 2 * lanes :])
            squashed = jnp.tanh(z)
            slopes = 1.0 - squashed * squashed
            slope[l, h] = slopes
            if l == LAYERS - 1:
                halo_put(LAYERS, h, slopes.astype(BF16).reshape(half, cols, lanes))
            before = x[l, own, :, 0:lanes].astype(F32)
            states = (before + squashed.reshape(half, cols, lanes)).astype(BF16)
            if l + 1 < LAYERS:
                halo_put(l + 1, h, states)
                x[l + 1, own, :, 0:lanes] = states
            else:
                xb[own, :, 0:lanes] = states

    heap = dot(q[...], xb[:, :, 0:lanes].reshape(nodes, lanes))
    score = jnp.sum(jnp.where(win_mask, heap * wide_readout, 0.0), axis=1, keepdims=True)
    flat = jnp.where(diag, score, 0.0)
    tile_row = iota((8, lanes), 0)
    tile = jnp.zeros((8, lanes), F32)
    for w in range(windows):
        part = jnp.sum(flat[w * cols : (w + 1) * cols], axis=0, keepdims=True)
        tile = jnp.where(tile_row == w, part, tile)
        count = jnp.sum(picked[w : w + 1], axis=1, keepdims=True)
        tile = jnp.where(tile_row == windows + w, count, tile)
    lik_slots[0, me_sta] = tile
    lik_slots[0, me_sta, 2 * windows : 3 * windows, 0:rows] = picked
    lik_slots[0, me_sta, 3 * windows : 4 * windows, 0:cols] = targets[...]

    def tile_copy(slot, d):
        return pltpu.make_async_remote_copy(
            src_ref=lik_slots.at[0, me_sta],
            dst_ref=lik_slots.at[slot, me_sta],
            send_sem=lik_send.at[slot, d],
            recv_sem=lik_recv.at[slot, d],
            device_id={"sta": sta_peer(d), "src": me_src + (0, 1, -1)[slot]},
            device_id_type=MESH,
        )

    def tiles(act, coming):
        for d in range(1, n_sta):
            act(tile_copy(0, d))
        for slot, side in ((1, 2 if coming else 3), (2, 3 if coming else 2)):

            @pl.when(sides[side])
            def _():
                for d in range(n_sta):
                    act(tile_copy(slot, d))

    tiles(lambda copy: copy.start(), False)
    halo_wait(LAYERS, range(2 + 2 * HALVES))
    halo_drain(LAYERS)
    tiles(lambda copy: copy.wait_recv(), True)

    lane_window = over(iota((8, lanes), 1), feature)

    def turn(values, row):
        return dot_tn(values, jnp.where(tile_row == row + lane_window, 1.0, 0.0))

    def error_of(slot):
        summed = lik_slots[slot, 0]
        for s in range(1, n_sta):
            summed = summed + lik_slots[slot, s]
        root = jnp.sqrt(jnp.maximum(summed[windows : 2 * windows], 1.0))
        lik = summed[0:windows] / root
        want = lik_slots[slot, 0, 3 * windows : 4 * windows]
        err = (jax.nn.sigmoid(lik) - want).astype(BF16).astype(F32)
        err = jnp.concatenate([err, jnp.zeros((8 - windows, lanes), F32)], axis=0)
        return lik, turn(err, 0)[:cols]

    lik, err_own = error_of(0)
    lik_out[...] = lik[:, :cols]
    outs = [pltpu.make_async_copy(lik_out, lik_hbm, out_sem.at[HALVES])]
    outs[0].start()
    heap_own = jnp.where(win_mask, heap, 0.0)
    heap_sum = heap_own[0:cols]
    for w in range(1, windows):
        heap_sum = heap_sum + heap_own[w * cols : (w + 1) * cols]
    v_row = jnp.sum(err_own * heap_sum, axis=0, keepdims=True)
    err_own = err_own * wide_readout
    err_left = error_of(1)[1][cols - HW :] * wide_readout
    err_right = error_of(2)[1][:HW] * wide_readout
    picks_own = turn(lik_slots[0, me_sta], 2 * windows)
    picks_up = turn(lik_slots[0, sta_peer(n_sta - 1)], 2 * windows)
    picks_down = turn(lik_slots[0, sta_peer(1)], 2 * windows)

    top = LAYERS

    def put_delta(l, h, grad):
        delta = (grad * slope[l, h]).astype(BF16).reshape(half, cols, lanes)
        if l == LAYERS - 1:
            hr[top, h * half : (h + 1) * half, HW : HW + cols] = delta
            hs[top, HW + h * half : HW + (h + 1) * half] = delta
        else:
            halo_put(2 * LAYERS - 1 - l, h, delta)
        xb[h * half : (h + 1) * half, :, 0:lanes] = delta

    def scaled(values, err, picked_row):
        return (values.astype(F32) * (err * picked_row)).astype(BF16)

    grads = []
    for h in range(HALVES):
        spots = range(h * half, (h + 1) * half)
        grads.append(jnp.concatenate([err_own * picks_own[i : i + 1] for i in spots], axis=0))
        put_delta(LAYERS - 1, h, grads[h])
    def rim_deltas(h):
        for m in range(HW):
            if h == 0:
                up = picks_up[rows - HW + m : rows - HW + m + 1]
                hs[top, m] = scaled(hs[top, m], err_own, up)
            else:
                down = picks_down[m : m + 1]
                hs[top, HW + rows + m] = scaled(hs[top, HW + rows + m], err_own, down)
        for i in range(h * half, (h + 1) * half):
            own_row = picks_own[i : i + 1]
            hr[top, i, 0:HW] = scaled(hr[top, i, 0:HW], err_left, own_row)
            hr[top, i, HW + cols :] = scaled(hr[top, i, HW + cols :], err_right, own_row)

    def weight_sums(l):
        delta = hs[2 * LAYERS - 1 - l, HW : HW + rows].reshape(nodes, lanes)
        w_t = dot_tn(delta, x[l].reshape(nodes, 3 * lanes))
        folded = []
        for p in range(3):
            both = jnp.where(
                first_window,
                w_t[0:feature, p * lanes : (p + 1) * lanes],
                w_t[feature:, p * lanes : (p + 1) * lanes],
            )
            folded.append(both + pltpu.roll(both, feature, 1))
        base = l * feature
        w_local[base : base + feature] = jnp.where(first_window, folded[0], folded[1])
        return folded[2]

    def chunk_of(ref, s):
        return ref.at[pl.ds(pl.multiple_of(s * chunk, 16), chunk)]

    first, second, third = [], [], []
    for l in reversed(range(LAYERS)):
        e = 2 * LAYERS - 1 - l
        if l == 0:
            kept = weight_sums(1)
            w_local[2 * feature : 3 * feature] = jnp.where(first_window, weight_sums(l), kept)
            w_local[3 * feature :] = jnp.broadcast_to(v_row, (w_local.shape[0] - 3 * feature, lanes))
            for d in range(1, n_sta):
                first.append(
                    pltpu.make_async_remote_copy(
                        src_ref=chunk_of(w_local, sta_peer(d)),
                        dst_ref=sta_slots.at[me_sta],
                        send_sem=a_send.at[d],
                        recv_sem=a_recv.at[d],
                        device_id={"sta": sta_peer(d)},
                        device_id_type=MESH,
                    )
                )
                first[-1].start()
            sta_slots[me_sta] = chunk_of(w_local, me_sta)[...]
        for h in range(HALVES):
            own = slice(h * half, (h + 1) * half)
            if e > top:
                halo_wait(e, (1 - h,))
            else:
                rim_deltas(h)
            mix_sta(1, e, h, xb)
            if l == 0 and h == 0:
                for copy in first:
                    copy.wait_recv()
                some = sta_slots[0]
                for s in range(1, n_sta):
                    some = some + sta_slots[s]
                src_slots[me_src] = some.astype(BF16)
                for d in range(1, n_src):
                    second.append(
                        pltpu.make_async_remote_copy(
                            src_ref=src_slots.at[me_src],
                            dst_ref=src_slots.at[me_src],
                            send_sem=b_send.at[d],
                            recv_sem=b_recv.at[d],
                            device_id={"src": src_peer(d)},
                            device_id_type=MESH,
                        )
                    )
                    second[-1].start()
            early = xb[own, :, 0 : 2 * lanes].reshape(part_nodes, 2 * lanes)
            grad = grads[h] + dot(early, wf[1, l, 0 : 2 * lanes])
            if e > top:
                halo_wait(e, (2 + 2 * h, 3 + 2 * h))
            mix_src(1, e, h, xb)
            late = xb[own, :, 2 * lanes :].reshape(part_nodes, lanes)
            grad = grad + dot(late, wf[1, l, 2 * lanes :])
            if l > 0:
                grads[h] = grad
                put_delta(l - 1, h, grad)
            else:
                grad_out[own] = grad.reshape(half, cols, lanes).astype(BF16)
                outs.append(pltpu.make_async_copy(grad_out.at[own], grad_hbm.at[own], out_sem.at[h]))
                outs[-1].start()

    for copy in second:
        copy.wait_recv()
    some = src_slots[0].astype(F32)
    for s in range(1, n_src):
        some = some + src_slots[s].astype(F32)
    chunk_of(total, me_sta)[...] = some
    for d in range(1, n_sta):
        third.append(
            pltpu.make_async_remote_copy(
                src_ref=chunk_of(total, me_sta),
                dst_ref=chunk_of(total, me_sta),
                send_sem=c_send.at[d],
                recv_sem=c_recv.at[d],
                device_id={"sta": sta_peer(d)},
                device_id_type=MESH,
            )
        )
        third[-1].start()
    for e in range(2 * LAYERS):
        if e != top:
            halo_drain(e)
    tiles(lambda copy: copy.wait_send(), False)
    for copy in first + second:
        copy.wait_send()
    for copy in third:
        copy.wait_recv()
    outs.append(pltpu.make_async_copy(total, w_hbm, out_sem.at[HALVES + 1]))
    outs[-1].start()
    for copy in third:
        copy.wait_send()
    for copy in outs:
        copy.wait()


def finish(factor, lik, grad, w_sum, lik_out, grad_out, w_out, v_out, lik_buf, grad_buf, sums, sems):
    loads = [
        pltpu.make_async_copy(src, dst, sems.at[0, n])
        for n, (src, dst) in enumerate(((grad, grad_buf), (w_sum, sums), (lik, lik_buf)))
    ]
    stores = [
        pltpu.make_async_copy(src, dst, sems.at[1, n])
        for n, (src, dst) in enumerate(((grad_buf, grad_out), (lik_buf, lik_out)))
    ]
    for copy in loads:
        copy.start()
    loads[0].wait()
    stores[0].start()
    loads[2].wait()
    stores[1].start()
    loads[1].wait()
    feature = w_out.shape[-1]
    for t in range(3):
        turned = jnp.transpose(sums[t * feature : (t + 1) * feature] * factor)
        for n in range(2):
            l, p = (t, n) if t < 2 else (n, 2)
            w_out[l, p] = turned[n * feature : (n + 1) * feature]
    row = sums[3 * feature : 3 * feature + 1] * factor
    v_out[...] = (row + pltpu.roll(row, feature, 1))[:, :feature]
    for copy in stores:
        copy.wait()


def shards(
    n_sta,
    n_src,
    features,
    station_lists,
    station_counts,
    source_lists,
    source_counts,
    picks,
    targets,
    layer_weights,
    readout_vector,
):
    rows, cols, lanes = features.shape
    feature = layer_weights.shape[-1]
    windows = lanes // feature
    nodes = rows * cols
    half = rows // HALVES
    span_s, span_r = rows + 2 * HW, cols + 2 * HW
    chunk = -(-(3 * feature + 1) // (16 * n_sta)) * 16
    w_rows = chunk * n_sta
    jw = windows * cols
    dma = pltpu.SemaphoreType.DMA
    hbm = pl.BlockSpec(memory_space=pl.ANY)
    vmem = pl.BlockSpec(memory_space=pltpu.VMEM)
    operands = (
        features,
        station_lists.T,
        station_counts.reshape(1, -1),
        source_lists.T,
        source_counts.reshape(1, -1),
        picks,
        targets,
        layer_weights,
        readout_vector.reshape(1, -1),
    )
    lik, grad, w_sum = pl.pallas_call(
        functools.partial(kernel, n_sta, n_src, chunk),
        out_shape=(
            jax.ShapeDtypeStruct((windows, cols), F32),
            jax.ShapeDtypeStruct((rows, cols, lanes), BF16),
            jax.ShapeDtypeStruct((w_rows, lanes), F32),
        ),
        in_specs=[hbm] * 9,
        out_specs=(hbm,) * 3,
        scratch_shapes=[pltpu.VMEM(a.shape, a.dtype) for a in operands[1:]]
        + [
            pltpu.VMEM((windows, cols), F32),
            pltpu.VMEM((rows, cols, lanes), BF16),
            pltpu.VMEM((2 * LAYERS, span_s, cols, lanes), BF16),
            pltpu.VMEM((2 * LAYERS, rows, span_r, lanes), BF16),
            pltpu.VMEM((LAYERS, rows, cols, 3 * lanes), BF16),
            pltpu.VMEM((rows, cols, 3 * lanes), BF16),
            pltpu.VMEM((LAYERS, HALVES, nodes // HALVES, lanes), F32),
            pltpu.VMEM((2, HALVES, half * J, (half + 2 * HW) * J), BF16),
            pltpu.VMEM((2, G * cols, G * span_r), BF16),
            pltpu.VMEM((2, LAYERS, 3 * lanes, lanes), BF16),
            pltpu.VMEM((jw, nodes), BF16),
            pltpu.VMEM((3, n_sta, 8, lanes), F32),
            pltpu.VMEM((w_rows, lanes), F32),
            pltpu.VMEM((n_sta, chunk, lanes), F32),
            pltpu.VMEM((n_src, chunk, lanes), BF16),
            pltpu.VMEM((w_rows, lanes), F32),
            dma((9,)),
            dma((HALVES + 2,)),
            dma((2 * LAYERS, 2 + 2 * HALVES)),
            dma((2 * LAYERS, 2 + 2 * HALVES)),
            dma((3, n_sta)),
            dma((3, n_sta)),
            dma((n_sta,)),
            dma((n_sta,)),
            dma((n_src,)),
            dma((n_src,)),
            dma((n_sta,)),
            dma((n_sta,)),
        ],
        compiler_params=pltpu.CompilerParams(
            collective_id=0, has_side_effects=True, vmem_limit_bytes=VMEM
        ),
    )(*operands)
    factor = float(1.0 / np.sqrt(np.float32(rows * n_sta * cols * n_src)))
    lik, grad, w_total, v_total = pl.pallas_call(
        functools.partial(finish, factor),
        out_shape=(
            jax.ShapeDtypeStruct(lik.shape, F32),
            jax.ShapeDtypeStruct(grad.shape, BF16),
            jax.ShapeDtypeStruct(layer_weights.shape, F32),
            jax.ShapeDtypeStruct((1, feature), F32),
        ),
        in_specs=[hbm] * 3,
        out_specs=(hbm, hbm, vmem, vmem),
        scratch_shapes=[
            pltpu.VMEM(lik.shape, F32),
            pltpu.VMEM(grad.shape, BF16),
            pltpu.VMEM(w_sum.shape, F32),
            dma((2, 3)),
        ],
        compiler_params=pltpu.CompilerParams(vmem_limit_bytes=VMEM),
    )(lik, grad, w_sum)
    return (lik, grad, w_total, v_total.reshape(feature))


def solution(mesh):
    in_specs = (P("sta", "src", None), P(), P(), P(), P(), P(None, "sta"), P(None, "src"), P(), P())
    out_specs = (P(None, "src"), P("sta", "src", None), P(), P())
    body = functools.partial(shards, mesh.shape["sta"], mesh.shape["src"])
    return jax.shard_map(body, mesh=mesh, in_specs=in_specs, out_specs=out_specs, check_vma=False)
```
